32 devices in a mesh: brain: 2 (over x), slab: 16 (over z, y, core).
Axes of the slice: x: 2, y: 2, z: 4, core: 2. Of those that a mesh axis runs over, the one named last changes fastest.
Arguments:
- features: bfloat16 [32, 192, 16, 128], P(None, ('brain', 'slab')), parts along dimension 1, may hold values from -6 to 6
- conv_weight: bfloat16 [3, 128, 288], replicated, may hold values from -0.21875 to 0.21875
- norm_gain: float32 [4, 32], replicated, may hold values from 0.25 to 1.75
- norm_bias: float32 [4, 32], replicated, may hold values from -3 to 3
- head_weight: bfloat16 [4, 6, 32], replicated, may hold values from -2 to 2
- head_bias: float32 [4, 6], replicated, may hold values from -4 to 308
- patch_offsets: int32 [32, 2], P(('brain', 'slab')), parts along dimension 0, may hold values from -2 to 2
- fg_mask: int32 [32, 2], P(('brain', 'slab')), parts along dimension 0, may hold values 0 or 1
- acq_counts: int32 [32], P(('brain', 'slab')), parts along dimension 0, may hold values from 1 to 8, 64 in all
Outputs:
- resampled: float32 [6, 256, 16, 128], P(None, ('brain', 'slab')), parts along dimension 1
The draws below stay inside these ranges and needn't reach their ends.
There are 2 independent parts, one for each index of `brain`. The reference program is written for one: setup_inputs(seed, part) draws one part's arguments, and reference() takes and returns one part's arrays. A program takes and returns all parts, laid end to end along the dimension named above; an argument that names none is the same for every part. Nothing has to cross between parts.
Inputs may be any that keep to these rules, and one draw needn't show every extreme that they name: `acq_counts`: within each brain volume separately, the 16 counts of that volume sum to 64 and some slab of that volume has exactly 8; the array of all volumes together sums to 64 once for every volume.
All inputs are finite; a program needn't handle non-finite values. No bound on the sum of `fg_mask` or of `acq_counts` on one device may be relied on, other than what follows from the above.
Results may differ from the reference program's by a relative error of at most 0.0003.
Values may be sent and summed in bfloat16 or wider, within the bound.
A program may use at most 64 MiB of HBM per device.

```python
import math
import jax
import jax.numpy as jnp
import numpy as np
from jax import lax

CHANNELS = 32
CLASSES = 6
FOLDS = 4
SLAB_X = 6
MARGIN = 2
JITTER = 2
PATCHES = 2
PATCH_ROWS = 8
COLUMNS = 128
RIM = 4
PATCH_X = 10
ROWS = 16
SLABS = 16
VOLUME_X = 96
ACQ_DEV = 4
MOST_ACQ = 8


def draw_head_bias(key, part):
    biases = jnp.clip(jax.random.normal(key, (FOLDS, CLASSES), jnp.float32), -4.0, 4.0)
    return biases


def with_ends(result, rng, least, top_value):
    dims = result.shape
    place = [jax.random.randint(jax.random.fold_in(rng, axis), (), 0, dims[axis]) for axis in range(len(dims))]
    result = result.at[tuple(place)].set(least)
    longest = dims.index(max(dims))
    place[longest] = (place[longest] + 1) % dims[longest]
    return result.at[tuple(place)].set(top_value)


def levels(key, dims, cuts, smallest, largest):
    factor_of = 1.0
    for position, shards_of in cuts:
        draws = jax.random.uniform(jax.random.fold_in(jax.random.fold_in(key, 6), position), (shards_of,), jnp.float32, smallest / len(cuts), largest / len(cuts))
        factor_of = factor_of * jnp.repeat(jnp.exp(draws), dims[position] // shards_of).reshape((-1,) + (1,) * (len(dims) - 1 - position))
    return factor_of


def profile(amount, total, most, slope):
    weights = [(1 << 20) // math.isqrt(grade ** slope) + 1 for grade in range(2, amount + 1)]
    spare, given = total - most - (amount - 1), [1] * (amount - 1)
    while spare > 0:
        free = [i for i in range(amount - 1) if given[i] < most]
        pool, remaining = sum([weights[i] for i in free]), spare
        for i in free:
            addition = min(most - given[i], max(1, remaining * weights[i] // pool), spare)
            given[i] = given[i] + addition
            spare = spare - addition
    return np.array([most] + given)


def uneven(rng, amount, total, most, skew):
    if amount == 2:
        one = jax.random.randint(rng, (), max(1, total - most), min(most, total - 1) + 1)
        return jnp.stack([one, total - one])
    lengths = jnp.asarray(profile(amount, total, most, skew), jnp.int32)
    couples = (amount - 1) // 2
    source_of, sink = lengths[1:1 + 2 * couples:2], lengths[2:2 + 2 * couples:2]
    margin = jnp.minimum(source_of - 1, most - sink)
    passed = jax.random.randint(jax.random.fold_in(rng, 1), (couples,), 0, 1 << 20) % (margin + 1)
    lengths = lengths.at[1:1 + 2 * couples:2].set(source_of - passed).at[2:2 + 2 * couples:2].set(sink + passed)
    return lengths[jax.random.permutation(jax.random.fold_in(rng, 2), amount)]


def gaussian(stream_key, shape, scale, bound, cuts=(), kind=jnp.bfloat16):
    level = levels(stream_key, shape, cuts, -0.22, 0.18) if cuts else 1.0
    result = jax.random.normal(stream_key, shape, jnp.float32) * scale * level
    return jnp.minimum(jnp.maximum(result, -bound), bound).astype(kind)


def setup_inputs(seed: int = 0, part: int = 0) -> dict:
    key_list = jax.random.split(jax.random.key(seed), 10)
    part_splits = jax.random.split(jax.random.fold_in(key_list[9], part), 10)
    return {
        "features": gaussian(part_splits[0], (CHANNELS, VOLUME_X, ROWS, COLUMNS), 1.0, 6.0, ((1, 16),)),
        "conv_weight": gaussian(key_list[1], (3, FOLDS * CHANNELS, 9 * CHANNELS), (27 * CHANNELS) ** -0.5, 0.21875),
        "norm_gain": jnp.clip(1.0 + 0.15 * jax.random.normal(key_list[2], (FOLDS, CHANNELS), jnp.float32), 0.25, 1.75),
        "norm_bias": gaussian(key_list[3], (FOLDS, CHANNELS), 0.7, 3.0, (), jnp.float32),
        "head_weight": gaussian(key_list[4], (FOLDS, CLASSES, CHANNELS), (CHANNELS // 4) ** -0.5, 2.0),
        "head_bias": draw_head_bias(jax.random.fold_in(key_list[9], 71), part),
        "patch_offsets": with_ends(jax.random.randint(part_splits[6], (SLABS, PATCHES), 0 - JITTER, JITTER + 1), jax.random.fold_in(part_splits[6], 1), 0 - JITTER, JITTER).astype(jnp.int32),
        "fg_mask": with_ends((jax.random.randint(part_splits[7], (SLABS, PATCHES), 0, 4) < 3).astype(jnp.int32), jax.random.fold_in(part_splits[7], 1), 0, 1),
        "acq_counts": uneven(part_splits[8], SLABS, ACQ_DEV * SLABS, MOST_ACQ, 1).astype(jnp.int32),
    }


prior_weight = 0.1

def gauss_line(length):
    positions = jnp.arange(length, dtype=jnp.float32)
    centre = (length - 1) / 2.0
    spread = length / 4.0
    scaled = (positions - centre) / spread
    return jnp.exp(-0.5 * scaled * scaled)

def patch_scores(patch, conv_weight, norm_gain, norm_bias, head_weight, head_bias):
    channels, length, row_span, column_count = patch.shape
    padded = jnp.pad(patch, ((0, 0), (1, 1), (1, 1), (0, 0)))
    zero_col = jnp.zeros(padded.shape[:-1] + (1,), padded.dtype)
    shifted = (jnp.concatenate([zero_col, padded[..., :-1]], -1), padded, jnp.concatenate([padded[..., 1:], zero_col], -1))
    tap_list = [source[:, :, row_shift:row_shift + row_span] for row_shift in range(3) for source in shifted]
    stacked = jnp.concatenate(tap_list, 0)
    conv_out = jnp.zeros((conv_weight.shape[1], length * row_span * column_count), jnp.float32)
    for depth_tap in range(3):
        sliced = stacked[:, depth_tap:depth_tap + length].reshape(9 * channels, -1)
        conv_out = conv_out + jnp.dot(conv_weight[depth_tap], sliced, preferred_element_type=jnp.float32)
    centre_mean = lax.optimization_barrier(jnp.mean(conv_out, axis=1, keepdims=True))
    centred = conv_out - centre_mean
    variance = lax.optimization_barrier(jnp.mean(centred * centred, axis=1, keepdims=True))
    normed = centred * lax.rsqrt(variance + 1e-05) * norm_gain.reshape(-1)[:, None] + norm_bias.reshape(-1)[:, None]
    activated = jnp.where(normed > 0, normed, 0.01 * normed)
    fold_count = head_weight.shape[0]
    logits = jnp.einsum('fkc,fcv->fkv', head_weight.astype(jnp.float32), activated.reshape(fold_count, channels, -1).astype(jnp.float32), precision=lax.Precision.HIGHEST) + head_bias[:, :, None]
    class_probs = lax.optimization_barrier(jnp.sum(jax.nn.softmax(logits, axis=1), axis=0)) / fold_count
    window = (gauss_line(length)[:, None, None] * gauss_line(row_span)[None, :, None] * gauss_line(column_count)[None, None, :]).reshape(-1)
    weighted = (class_probs * window[None, :]).reshape(-1, length, row_span, column_count)
    return (weighted, window.reshape(length, row_span, column_count))

def reference(features, conv_weight, norm_gain, norm_bias, head_weight, head_bias, patch_offsets, fg_mask, acq_counts):
    channels, volume, row_total, column_count = features.shape
    padded = jnp.pad(features, ((0, 0), (RIM, RIM), (0, 0), (0, 0)))
    prob_init = jnp.zeros((CLASSES, volume + 2 * RIM, row_total, column_count), jnp.float32)
    weight_init = jnp.zeros((volume + 2 * RIM, row_total, column_count), jnp.float32)
    zero_index = jnp.zeros((), jnp.int32)

    def one_slab(carry, slab_id):
        prob_sums, weight_sums = carry
        for patch_index in range(PATCHES):
            row_first = patch_index * PATCH_ROWS
            row_index = jnp.asarray(row_first, jnp.int32)
            patch_start = (slab_id * SLAB_X + RIM - MARGIN + patch_offsets[slab_id, patch_index]).astype(jnp.int32)
            patch = lax.dynamic_slice_in_dim(padded[:, :, row_first:row_first + PATCH_ROWS], patch_start, PATCH_X, 1)
            class_probs, window = patch_scores(patch, conv_weight, norm_gain, norm_bias, head_weight, head_bias)
            keep_value = fg_mask[slab_id, patch_index].astype(jnp.float32)
            old_probs = lax.dynamic_slice(prob_sums, (zero_index, patch_start, row_index, zero_index), class_probs.shape)
            prob_sums = lax.dynamic_update_slice(prob_sums, old_probs + class_probs * keep_value, (zero_index, patch_start, row_index, zero_index))
            old_weights = lax.dynamic_slice(weight_sums, (patch_start, row_index, zero_index), window.shape)
            weight_sums = lax.dynamic_update_slice(weight_sums, old_weights + window * keep_value, (patch_start, row_index, zero_index))
        return ((prob_sums, weight_sums), None)
    (prob_sums, weight_sums), unused = lax.scan(one_slab, (prob_init, weight_init), jnp.arange(SLABS, dtype=jnp.int32))
    background = (jnp.arange(CLASSES) == 0).astype(jnp.float32)[:, None, None, None] * prior_weight
    merged = (prob_sums[:, RIM:RIM + volume] + background) / (weight_sums[RIM:RIM + volume] + prior_weight)
    edged = jnp.pad(merged, ((0, 0), (1, 1), (0, 0), (0, 0)))

    def resample(slab_id):
        acq_count = acq_counts[slab_id].astype(jnp.float32)
        slot_ids = jnp.arange(MOST_ACQ, dtype=jnp.float32)
        step_size = SLAB_X / jnp.maximum(acq_count - 1.0, 1.0)
        local_pos = slot_ids * step_size - 0.5
        slab_anchor = (slab_id * SLAB_X).astype(jnp.float32)
        global_pos = jnp.clip(slab_anchor + local_pos, 0.0, float(volume - 1))
        local_pos = global_pos - slab_anchor
        plane_pos = jnp.arange(SLAB_X + 2, dtype=jnp.float32) - 1.0
        used = (slot_ids < acq_count).astype(jnp.float32)
        resample_matrix = jnp.maximum(0.0, 1.0 - jnp.abs(local_pos[:, None] - plane_pos[None, :])) * used[:, None]
        planes_near = lax.dynamic_slice_in_dim(edged, (slab_id * SLAB_X).astype(jnp.int32), SLAB_X + 2, 1)
        return jnp.einsum('kj,cjhw->ckhw', resample_matrix, planes_near, precision=lax.Precision.HIGHEST)
    stacked = lax.map(resample, jnp.arange(SLABS, dtype=jnp.int32))
    return jnp.transpose(stacked, (1, 0, 2, 3, 4)).reshape(CLASSES, SLABS * MOST_ACQ, row_total, column_count)
```

```python
import functools

import jax
import jax.numpy as jnp
from jax import lax
from jax.experimental import pallas as pl
from jax.experimental.pallas import tpu as pltpu
from jax.sharding import PartitionSpec as P

MARGIN = 2
RIM = 4
PATCH_X = 10
MOST_ACQ = 8
PRIOR = 0.1
EDGE = RIM + 1
BF = jnp.bfloat16
F32 = jnp.float32


def iota(shape, dim):
    return lax.broadcasted_iota(jnp.int32, shape, dim)


def gauss(index, length):
    scaled = (index - (length - 1) / 2.0) / (length / 4.0)
    return jnp.exp(-0.5 * scaled * scaled)


def kernel(
    feat, wts, gain_ref, bias_ref, head_ref, hbias_ref, offs, keep_ref, acq,
    out,
    before, after, xs, wcat, conv, wpad, snd_lo, snd_hi, rcv_below, rcv_above,
    stat, coef, halo_send, halo_recv, edge_send, edge_recv,
):
    channels, planes, rows, cols = feat.shape
    folds, classes, _ = head_ref.shape
    patches = offs.shape[1]
    prow = rows // patches
    wide = folds * channels
    half = channels // 2
    slabs = lax.axis_size("slab")
    me = lax.axis_index("slab")
    has_left, has_right = me > 0, me < slabs - 1
    left, right = {"slab": me - 1}, {"slab": me + 1}

    barrier = pltpu.get_barrier_semaphore()

    @pl.when(has_left)
    def _():
        pl.semaphore_signal(barrier, inc=1, device_id=left)

    @pl.when(has_right)
    def _():
        pl.semaphore_signal(barrier, inc=1, device_id=right)

    interior = has_left & has_right

    @pl.when(interior)
    def _():
        pl.semaphore_wait(barrier, 2)

    @pl.when(jnp.logical_not(interior))
    def _():
        pl.semaphore_wait(barrier, 1)

    def remote(src, dst, sems, slot, target):
        return pltpu.make_async_remote_copy(
            src_ref=src, dst_ref=dst, send_sem=sems[0].at[slot], recv_sem=sems[1].at[slot],
            device_id=target,
        )

    halo = (halo_send, halo_recv)
    edge = (edge_send, edge_recv)
    halo_right = remote(feat.at[:, planes - RIM :], before, halo, 0, right)
    halo_left = remote(feat.at[:, :RIM], after, halo, 1, left)

    @pl.when(has_right)
    def _():
        halo_right.start()

    @pl.when(has_left)
    def _():
        halo_left.start()

    @pl.when(me == 0)
    def _():
        before[...] = jnp.zeros_like(before)
        rcv_below[...] = jnp.zeros_like(rcv_below)

    @pl.when(me == slabs - 1)
    def _():
        after[...] = jnp.zeros_like(after)
        rcv_above[...] = jnp.zeros_like(rcv_above)

    depth = wts.shape[2]
    for a in range(3):
        wcat[:, a * depth : (a + 1) * depth] = wts[a]
    eye = iota((channels, channels), 0) == iota((channels, channels), 1)

    def column(values):
        return jnp.concatenate(
            [
                jnp.sum(jnp.where(eye, values[f : f + 1, :], 0.0), axis=1, keepdims=True)
                for f in range(folds)
            ],
            axis=0,
        )

    gain_col = column(gain_ref[...])
    bias_col = column(bias_ref[...])
    heads = folds * classes
    head_row = iota((heads, wide), 0)
    head_lane = iota((heads, wide), 1)
    head = jnp.zeros((heads, wide), F32)
    for f in range(folds):
        tiled = jnp.concatenate([head_ref[f].astype(F32)] * folds, axis=1)
        for k in range(classes):
            here = (head_row == k * folds + f) & (head_lane // channels == f)
            head = jnp.where(here, tiled[k : k + 1, :], head)
    head2 = jnp.concatenate([head, head], axis=1).astype(BF)
    hb = jnp.concatenate([hbias_ref[...]] * classes, axis=0)
    pick = iota((heads, classes), 0) // folds == iota((heads, classes), 1)
    head_bias = jnp.sum(jnp.where(pick, hb, 0.0), axis=1, keepdims=True)

    m_i, k_i = iota((half * rows, half * rows), 0), iota((half * rows, half * rows), 1)
    swap = (k_i == (m_i % half) * rows + m_i // half).astype(F32).astype(BF)
    stack = heads * prow
    m_i, k_i = iota((classes * prow, stack), 0), iota((classes * prow, stack), 1)
    gather = (k_i // heads == m_i % prow) & ((k_i % heads) // folds == m_i // prow)
    gather = gather.astype(F32)
    gather = jnp.concatenate([gather, gather], axis=1).astype(BF)

    starts = [RIM - MARGIN + offs[0, p] for p in range(patches)]
    lane = iota((half * rows, cols), 1)
    unit = 3 * channels
    zero_row = jnp.zeros((unit, cols), BF)

    def lay_planes(source, first, base, count, masked):
        @pl.loop(0, count // 2)
        def _(pair):
            pair_planes = [source[:, first + 2 * pair + e].reshape(channels * rows, cols) for e in range(2)]
            for g in range(2):
                part = jnp.concatenate(
                    [v[g * half * rows : (g + 1) * half * rows] for v in pair_planes], axis=1
                )
                turned = jnp.dot(swap, part, preferred_element_type=F32)
                for e in range(2):
                    j = base + 2 * pair + e
                    here = turned[:, e * cols : (e + 1) * cols]
                    taps = (
                        jnp.where(lane == 0, 0.0, pltpu.roll(here, 1, 1)),
                        here,
                        jnp.where(lane == cols - 1, 0.0, pltpu.roll(here, cols - 1, 1)),
                    )
                    for p in range(patches):
                        if masked:
                            inside = (j >= starts[p]) & (j < starts[p] + PATCH_X)
                            factor = jnp.where(inside, 1.0, 0.0)
                        for c, tap in enumerate(taps):
                            mine = tap[p * prow * half : (p + 1) * prow * half]
                            if masked:
                                mine = mine * factor
                            mine = mine.astype(BF)
                            for r in range(prow):
                                at = (r + 1) * unit + c * channels + g * half
                                xs[p, j + 1, at : at + half, :] = mine[r * half : (r + 1) * half]

    span = planes + 2 * RIM
    for p in range(patches):
        xs[p, 0] = jnp.zeros((xs.shape[2], cols), BF)
        xs[p, span + 1] = jnp.zeros((xs.shape[2], cols), BF)

        @pl.loop(1, span + 1)
        def _(j, p=p):
            xs[p, j, 0:unit, :] = zero_row
            xs[p, j, (prow + 1) * unit : (prow + 2) * unit, :] = zero_row

        for j in (*range(RIM), *range(RIM + PATCH_X, 2 * RIM + PATCH_X)):
            wpad[p, j] = jnp.zeros(wpad.shape[2:], F32)

    lay_planes(feat, 0, RIM, planes, False)

    @pl.when(has_left)
    def _():
        remote(feat.at[:, planes - RIM :], before, halo, 0, left).wait_recv()

    @pl.when(has_right)
    def _():
        remote(feat.at[:, :RIM], after, halo, 1, right).wait_recv()

    lay_planes(before, 0, 0, RIM, True)
    lay_planes(after, 0, RIM + planes, RIM, True)

    def conv_plane(p, i):
        x = starts[p] + i
        for pair in range(prow // 2):
            sides = []
            for h in (2 * pair, 2 * pair + 1):
                sides.append(
                    jnp.concatenate(
                        [xs[p, x + a, h * unit : h * unit + depth, :] for a in range(3)], axis=0
                    )
                )
            conv[p, i, :, 2 * pair * cols : (2 * pair + 2) * cols] = jnp.dot(
                wcat[...], jnp.concatenate(sides, axis=1), preferred_element_type=F32
            )

    def shift_of(p):
        total = conv[p, 0, :, 0:cols]
        for h in range(1, prow):
            total = total + conv[p, 0, :, h * cols : (h + 1) * cols]
        mean = jnp.sum(total, axis=1, keepdims=True) * (1.0 / (prow * cols))
        stat[p, 0] = jnp.broadcast_to(mean, (wide, cols))
        stat[p, 1] = jnp.zeros((wide, cols), F32)
        stat[p, 2] = jnp.zeros((wide, cols), F32)

    def add_stats(p, i):
        for lo in range(0, wide, 32):
            rows_here = slice(lo, lo + 32)
            base = stat[p, 0, rows_here]
            first, second = stat[p, 1, rows_here], stat[p, 2, rows_here]
            for h in range(prow):
                d = conv[p, i, rows_here, h * cols : (h + 1) * cols] - base
                first = first + d
                second = second + d * d
            stat[p, 1, rows_here] = first
            stat[p, 2, rows_here] = second

    def affine(p):
        size = 1.0 / (PATCH_X * prow * cols)
        d_mean = jnp.sum(stat[p, 1], axis=1, keepdims=True) * size
        var = jnp.sum(stat[p, 2], axis=1, keepdims=True) * size - d_mean * d_mean
        scale = lax.rsqrt(jnp.maximum(var, 0.0) + 1e-05) * gain_col
        mean = stat[p, 0][:, 0:1] + d_mean
        return scale, bias_col - mean * scale

    row_f = iota((prow, cols), 0).astype(F32)
    col_f = iota((prow, cols), 1).astype(F32)
    flat = gauss(row_f, prow) * gauss(col_f, cols)

    def score_plane(p, i, scale, offset):
        blocks = []
        for pair in range(prow // 2):
            y = conv[p, i, :, 2 * pair * cols : (2 * pair + 2) * cols] * scale + offset
            y = jnp.maximum(y, 0.01 * y)
            big = y.astype(BF)
            small = (y - big.astype(F32)).astype(BF)
            logits = jnp.dot(
                head2, jnp.concatenate([big, small], axis=0), preferred_element_type=F32
            ) + head_bias
            groups = [logits[j : j + 8] for j in range(0, heads, 8)]
            top = functools.reduce(jnp.maximum, groups)
            top = jnp.maximum(top, pltpu.roll(top, 4, 0))
            exps = [jnp.exp(v - top) for v in groups]
            total = functools.reduce(jnp.add, exps)
            total = total + pltpu.roll(total, 4, 0)
            inverse = 1.0 / total
            probs = jnp.concatenate([v * inverse for v in exps], axis=0)
            blocks += [probs[:, :cols], probs[:, cols:]]
        tall = jnp.concatenate(blocks, axis=0)
        big = tall.astype(BF)
        small = (tall - big.astype(F32)).astype(BF)
        summed = jnp.dot(
            gather, jnp.concatenate([big, small], axis=0), preferred_element_type=F32
        )
        index = lax.convert_element_type(i, F32)
        keep = keep_ref[0, p].astype(F32)
        window = gauss(jnp.full((prow, cols), index, F32), PATCH_X) * flat * keep
        share = window * (1.0 / folds)
        for k in range(classes):
            wpad[p, RIM + i, k] = summed[k * prow : (k + 1) * prow] * share
        wpad[p, RIM + i, classes] = window

    def send_edges(p):
        for j in range(EDGE):
            snd_lo[p, j] = wpad[p, j - starts[p] + RIM]
            snd_hi[p, j] = wpad[p, RIM + planes - 1 + j - starts[p] + RIM]

        @pl.when(has_right)
        def _():
            remote(snd_hi.at[p], rcv_below.at[p], edge, 2 * p, right).start()

        @pl.when(has_left)
        def _():
            remote(snd_lo.at[p], rcv_above.at[p], edge, 2 * p + 1, left).start()

    conv_plane(0, 0)
    shift_of(0)
    add_stats(0, 0)

    @pl.loop(1, PATCH_X)
    def _(i):
        conv_plane(0, i)
        add_stats(0, i)

    for p in range(patches):
        scale, offset = affine(p)
        if p + 1 < patches:
            conv_plane(p + 1, 0)
            shift_of(p + 1)
            add_stats(p + 1, 0)
            score_plane(p, 0, scale, offset)

            @pl.loop(1, PATCH_X)
            def _(i, p=p, scale=scale, offset=offset):
                conv_plane(p + 1, i)
                score_plane(p, i, scale, offset)
                add_stats(p + 1, i)
        else:

            @pl.loop(0, PATCH_X)
            def _(i, p=p, scale=scale, offset=offset):
                score_plane(p, i, scale, offset)

        send_edges(p)

    shape = (prow, cols)
    count = jnp.full(shape, acq[0].astype(F32), F32)
    step = planes / jnp.maximum(count - 1.0, 1.0)
    anchor = jnp.full(shape, (me * planes).astype(F32), F32)
    last = (slabs * planes - 1) * 1.0
    for slot in range(MOST_ACQ):
        position = jnp.clip(anchor + (slot * step - 0.5), 0.0, last) - anchor
        for e in range(planes + 2):
            value = jnp.maximum(0.0, 1.0 - jnp.abs(position - (e - 1.0)))
            coef[slot, e] = jnp.where(count > slot, value, 0.0)

    for p in range(patches):

        @pl.when(has_right)
        def _():
            remote(snd_hi.at[p], rcv_below.at[p], edge, 2 * p, right).wait_send()
            remote(snd_lo.at[p], rcv_above.at[p], edge, 2 * p + 1, right).wait_recv()

        @pl.when(has_left)
        def _():
            remote(snd_lo.at[p], rcv_above.at[p], edge, 2 * p + 1, left).wait_send()
            remote(snd_hi.at[p], rcv_below.at[p], edge, 2 * p, left).wait_recv()

        def total(e, k):
            value = wpad[p, e + RIM - 1 - starts[p] + RIM, k]
            if e < EDGE:
                value = value + rcv_below[p, e, k]
            if e >= planes + 2 - EDGE:
                value = value + rcv_above[p, e - (planes + 2 - EDGE), k]
            return value

        inverses = [1.0 / (total(e, classes) + PRIOR) for e in range(planes + 2)]
        for k in range(classes):
            merged = []
            for e in range(planes + 2):
                value = total(e, k)
                if k == 0:
                    value = value + PRIOR
                merged.append(value * inverses[e])
            for slot in range(MOST_ACQ):
                value = coef[slot, 0] * merged[0]
                for e in range(1, planes + 2):
                    value = value + coef[slot, e] * merged[e]
                out[k, slot, p * prow : (p + 1) * prow, :] = value

    @pl.when(has_right)
    def _():
        halo_right.wait_send()

    @pl.when(has_left)
    def _():
        halo_left.wait_send()


def local(features, conv_weight, norm_gain, norm_bias, head_weight, head_bias, patch_offsets, fg_mask, acq_counts):
    channels, planes, rows, cols = features.shape
    folds, classes, _ = head_weight.shape
    patches = patch_offsets.shape[1]
    prow = rows // patches
    wide = folds * channels
    span = planes + 2 * RIM
    vmem = pl.BlockSpec(memory_space=pltpu.VMEM)
    smem = pl.BlockSpec(memory_space=pltpu.SMEM)
    edges = pltpu.VMEM((patches, EDGE, classes + 1, prow, cols), F32)
    cells = PATCH_X * prow * cols * patches
    return pl.pallas_call(
        kernel,
        out_shape=jax.ShapeDtypeStruct((classes, MOST_ACQ, rows, cols), F32),
        in_specs=[vmem] * 6 + [smem] * 3,
        out_specs=vmem,
        scratch_shapes=[
            pltpu.VMEM((channels, RIM, rows, cols), BF),
            pltpu.VMEM((channels, RIM, rows, cols), BF),
            pltpu.VMEM((patches, span + 2, (prow + 2) * 3 * channels, cols), BF),
            pltpu.VMEM((wide, 27 * channels), BF),
            pltpu.VMEM((patches, PATCH_X, wide, prow * cols), F32),
            pltpu.VMEM((patches, PATCH_X + 2 * RIM, classes + 1, prow, cols), F32),
            edges, edges, edges, edges,
            pltpu.VMEM((patches, 3, wide, cols), F32),
            pltpu.VMEM((MOST_ACQ, planes + 2, prow, cols), F32),
            pltpu.SemaphoreType.DMA((2,)),
            pltpu.SemaphoreType.DMA((2,)),
            pltpu.SemaphoreType.DMA((2 * patches,)),
            pltpu.SemaphoreType.DMA((2 * patches,)),
        ],
        compiler_params=pltpu.CompilerParams(
            collective_id=0, has_side_effects=True, vmem_limit_bytes=56 * 1024 * 1024
        ),
        cost_estimate=pl.CostEstimate(
            flops=2 * cells * wide * 27 * channels,
            bytes_accessed=2 * features.size + 4 * classes * MOST_ACQ * rows * cols,
            transcendentals=cells * folds * classes,
        ),
    )(features, conv_weight, norm_gain, norm_bias, head_weight, head_bias, patch_offsets, fg_mask, acq_counts)


def solution(mesh):
    whole = P(None, ("brain", "slab"), None, None)
    by_slab = P(("brain", "slab"), None)
    in_specs = (whole, P(), P(), P(), P(), P(), by_slab, by_slab, P(("brain", "slab")))
    return jax.shard_map(local, mesh=mesh, in_specs=in_specs, out_specs=whole, check_vma=False)
```

```python
import functools

import jax
import jax.numpy as jnp
from jax import lax
from jax.experimental import pallas as pl
from jax.experimental.pallas import tpu as pltpu
from jax.sharding import PartitionSpec as P

MARGIN = 2
RIM = 4
PATCH_X = 10
MOST_ACQ = 8
PRIOR = 0.1
EDGE = RIM + 1
BF = jnp.bfloat16
F32 = jnp.float32


def iota(shape, dim):
    return lax.broadcasted_iota(jnp.int32, shape, dim)


def gauss(index, length):
    scaled = (index - (length - 1) / 2.0) / (length / 4.0)
    return jnp.exp(-0.5 * scaled * scaled)


def kernel(
    feat, wts, gain_ref, bias_ref, head_ref, hbias_ref, offs, keep_ref, acq,
    out,
    before, after, xs, wcat, conv, wpad, snd_lo, snd_hi, rcv_below, rcv_above,
    stat, coef, halo_send, halo_recv, edge_send, edge_recv,
):
    channels, planes, rows, cols = feat.shape
    classes, folds, _ = head_ref.shape
    patches = offs.shape[1]
    prow = rows // patches
    wide = folds * channels
    half = channels // 2
    slabs = lax.axis_size("slab")
    me = lax.axis_index("slab")
    has_left, has_right = me > 0, me < slabs - 1
    left, right = {"slab": me - 1}, {"slab": me + 1}

    barrier = pltpu.get_barrier_semaphore()

    @pl.when(has_left)
    def _():
        pl.semaphore_signal(barrier, inc=1, device_id=left)

    @pl.when(has_right)
    def _():
        pl.semaphore_signal(barrier, inc=1, device_id=right)

    interior = has_left & has_right

    @pl.when(interior)
    def _():
        pl.semaphore_wait(barrier, 2)

    @pl.when(jnp.logical_not(interior))
    def _():
        pl.semaphore_wait(barrier, 1)

    def remote(src, dst, sems, slot, target):
        return pltpu.make_async_remote_copy(
            src_ref=src, dst_ref=dst, send_sem=sems[0].at[slot], recv_sem=sems[1].at[slot],
            device_id=target,
        )

    halo = (halo_send, halo_recv)
    edge = (edge_send, edge_recv)
    halo_right = remote(feat.at[:, planes - RIM :], before, halo, 0, right)
    halo_left = remote(feat.at[:, :RIM], after, halo, 1, left)

    @pl.when(has_right)
    def _():
        halo_right.start()

    @pl.when(has_left)
    def _():
        halo_left.start()

    @pl.when(me == 0)
    def _():
        before[...] = jnp.zeros_like(before)
        rcv_below[...] = jnp.zeros_like(rcv_below)

    @pl.when(me == slabs - 1)
    def _():
        after[...] = jnp.zeros_like(after)
        rcv_above[...] = jnp.zeros_like(rcv_above)

    depth = wts.shape[1]
    same = (iota((wide, wide), 0) == iota((wide, wide), 1)).astype(F32).astype(BF)
    wcat[...] = lax.dot_general(
        same, wts[...].reshape(3 * depth, wide), (((1,), (1,)), ((), ())), preferred_element_type=F32
    ).astype(BF)
    eye = iota((channels, channels), 0) == iota((channels, channels), 1)

    def column(values):
        return jnp.concatenate(
            [
                jnp.sum(jnp.where(eye, values[f : f + 1, :], 0.0), axis=1, keepdims=True)
                for f in range(folds)
            ],
            axis=0,
        )

    gain_col = column(gain_ref[...])
    bias_col = column(bias_ref[...])
    heads = folds * classes
    head_row = iota((heads, wide), 0)
    head_lane = iota((heads, wide), 1)
    flat_head = head_ref[...].astype(F32).reshape(heads, channels)
    head = jnp.concatenate([flat_head] * folds, axis=1)
    head = jnp.where(head_lane // channels == head_row % folds, head, 0.0)
    head2 = jnp.concatenate([head, head], axis=1).astype(BF)
    hb = jnp.concatenate([hbias_ref[...]] * classes, axis=0)
    pick = iota((heads, classes), 0) // folds == iota((heads, classes), 1)
    head_bias = jnp.sum(jnp.where(pick, hb, 0.0), axis=1, keepdims=True)

    m_i, k_i = iota((half * rows, half * rows), 0), iota((half * rows, half * rows), 1)
    swap = (k_i == (m_i % half) * rows + m_i // half).astype(F32).astype(BF)
    stack = heads * prow
    m_i, k_i = iota((classes * prow, stack), 0), iota((classes * prow, stack), 1)
    gather = (k_i // heads == m_i % prow) & ((k_i % heads) // folds == m_i // prow)
    gather = gather.astype(F32)
    gather = jnp.concatenate([gather, gather], axis=1).astype(BF)

    starts = [RIM - MARGIN + offs[0, p] for p in range(patches)]
    lane = iota((half * rows, cols), 1)
    unit = 3 * channels
    zero_row = jnp.zeros((unit, cols), BF)

    def lay_planes(source, first, base, count, masked):
        @pl.loop(0, count // 2)
        def _(pair):
            pair_planes = [source[:, first + 2 * pair + e].reshape(channels * rows, cols) for e in range(2)]
            for g in range(2):
                part = jnp.concatenate(
                    [v[g * half * rows : (g + 1) * half * rows] for v in pair_planes], axis=1
                )
                turned = jnp.dot(swap, part, preferred_element_type=F32)
                for e in range(2):
                    j = base + 2 * pair + e
                    here = turned[:, e * cols : (e + 1) * cols]
                    taps = (
                        jnp.where(lane == 0, 0.0, pltpu.roll(here, 1, 1)),
                        here,
                        jnp.where(lane == cols - 1, 0.0, pltpu.roll(here, cols - 1, 1)),
                    )
                    for p in range(patches):
                        if masked:
                            inside = (j >= starts[p]) & (j < starts[p] + PATCH_X)
                            factor = jnp.where(inside, 1.0, 0.0)
                        for c, tap in enumerate(taps):
                            mine = tap[p * prow * half : (p + 1) * prow * half]
                            if masked:
                                mine = mine * factor
                            mine = mine.astype(BF)
                            for r in range(prow):
                                at = (r + 1) * unit + c * channels + g * half
                                xs[p, j + 1, at : at + half, :] = mine[r * half : (r + 1) * half]

    span = planes + 2 * RIM
    for p in range(patches):
        xs[p, 0] = jnp.zeros((xs.shape[2], cols), BF)
        xs[p, span + 1] = jnp.zeros((xs.shape[2], cols), BF)

        @pl.loop(1, span + 1)
        def _(j, p=p):
            xs[p, j, 0:unit, :] = zero_row
            xs[p, j, (prow + 1) * unit : (prow + 2) * unit, :] = zero_row

        wpad[p, PATCH_X] = jnp.zeros(wpad.shape[2:], F32)

    lay_planes(feat, 0, RIM, planes, False)

    inner = planes - 2
    rest = PATCH_X - inner

    def rest_index(p, t):
        return t + jnp.where(starts[p] + t <= RIM, 0, inner)

    def conv_plane(p, i, x):
        for pair in range(prow // 2):
            sides = []
            for h in (2 * pair, 2 * pair + 1):
                sides.append(
                    jnp.concatenate(
                        [xs[p, x + a, h * unit : h * unit + depth, :] for a in range(3)], axis=0
                    )
                )
            conv[p, i, :, 2 * pair * cols : (2 * pair + 2) * cols] = jnp.dot(
                wcat[...], jnp.concatenate(sides, axis=1), preferred_element_type=F32
            )

    def shift_of(p):
        total = conv[p, 0, :, 0:cols]
        for h in range(1, prow):
            total = total + conv[p, 0, :, h * cols : (h + 1) * cols]
        mean = jnp.sum(total, axis=1, keepdims=True) * (1.0 / (prow * cols))
        stat[p, 0] = jnp.broadcast_to(mean, (wide, cols))
        stat[p, 1] = jnp.zeros((wide, cols), F32)
        stat[p, 2] = jnp.zeros((wide, cols), F32)

    def add_stats(p, i):
        for lo in range(0, wide, 32):
            rows_here = slice(lo, lo + 32)
            base = stat[p, 0, rows_here]
            first, second = stat[p, 1, rows_here], stat[p, 2, rows_here]
            for h in range(prow):
                d = conv[p, i, rows_here, h * cols : (h + 1) * cols] - base
                first = first + d
                second = second + d * d
            stat[p, 1, rows_here] = first
            stat[p, 2, rows_here] = second

    def affine(p):
        size = 1.0 / (PATCH_X * prow * cols)
        d_mean = jnp.sum(stat[p, 1], axis=1, keepdims=True) * size
        var = jnp.sum(stat[p, 2], axis=1, keepdims=True) * size - d_mean * d_mean
        scale = lax.rsqrt(jnp.maximum(var, 0.0) + 1e-05) * gain_col
        mean = stat[p, 0][:, 0:1] + d_mean
        return scale, bias_col - mean * scale

    row_f = iota((prow, cols), 0).astype(F32)
    col_f = iota((prow, cols), 1).astype(F32)
    flat = gauss(row_f, prow) * gauss(col_f, cols)

    def score_plane(p, i, index, scale, offset):
        blocks = []
        for pair in range(prow // 2):
            y = conv[p, i, :, 2 * pair * cols : (2 * pair + 2) * cols] * scale + offset
            y = jnp.maximum(y, 0.01 * y)
            big = y.astype(BF)
            small = (y - big.astype(F32)).astype(BF)
            logits = jnp.dot(
                head2, jnp.concatenate([big, small], axis=0), preferred_element_type=F32
            ) + head_bias
            groups = [logits[j : j + 8] for j in range(0, heads, 8)]
            top = functools.reduce(jnp.maximum, groups)
            top = jnp.maximum(top, pltpu.roll(top, 4, 0))
            exps = [jnp.exp(v - top) for v in groups]
            total = functools.reduce(jnp.add, exps)
            total = total + pltpu.roll(total, 4, 0)
            inverse = 1.0 / total
            probs = jnp.concatenate([v * inverse for v in exps], axis=0)
            blocks += [probs[:, :cols], probs[:, cols:]]
        tall = jnp.concatenate(blocks, axis=0)
        big = tall.astype(BF)
        small = (tall - big.astype(F32)).astype(BF)
        summed = jnp.dot(
            gather, jnp.concatenate([big, small], axis=0), preferred_element_type=F32
        )
        index = lax.convert_element_type(index, F32)
        keep = keep_ref[0, p].astype(F32)
        window = gauss(jnp.full((prow, cols), index, F32), PATCH_X) * flat * keep
        share = window * (1.0 / folds)
        for k in range(classes):
            wpad[p, i, k] = summed[k * prow : (k + 1) * prow] * share
        wpad[p, i, classes] = window

    def slot_of(p, j):
        if RIM < j < RIM + planes - 1:
            return j - RIM - 1
        i = j - starts[p]
        if j <= RIM:
            return jnp.where(i >= 0, inner + i, PATCH_X)
        return jnp.where(i < PATCH_X, i, PATCH_X)

    def send_edges(p):
        for j in range(EDGE):
            snd_lo[p, j] = wpad[p, slot_of(p, j)]
            snd_hi[p, j] = wpad[p, slot_of(p, RIM + planes - 1 + j)]

        @pl.when(has_right)
        def _():
            remote(snd_hi.at[p], rcv_below.at[p], edge, 2 * p, right).start()

        @pl.when(has_left)
        def _():
            remote(snd_lo.at[p], rcv_above.at[p], edge, 2 * p + 1, left).start()

    for p in range(patches):
        conv_plane(p, 0, RIM + 1)
        shift_of(p)
        add_stats(p, 0)

        @pl.loop(1, inner)
        def _(i, p=p):
            conv_plane(p, i, RIM + 1 + i)
            add_stats(p, i)

    @pl.when(has_left)
    def _():
        remote(feat.at[:, planes - RIM :], before, halo, 0, left).wait_recv()

    @pl.when(has_right)
    def _():
        remote(feat.at[:, :RIM], after, halo, 1, right).wait_recv()

    lay_planes(before, 0, 0, RIM, True)
    lay_planes(after, 0, RIM + planes, RIM, True)

    def conv_rest(p, t):
        conv_plane(p, inner + t, starts[p] + rest_index(p, t))
        add_stats(p, inner + t)

    def score_rest(p, t, norms):
        score_plane(p, inner + t, rest_index(p, t), *norms)

    @pl.loop(0, rest)
    def _(t):
        conv_rest(0, t)

    norms = []
    for p in range(patches):
        norms.append(affine(p))

        @pl.loop(0, rest)
        def _(t, p=p):
            if p + 1 < patches:
                conv_rest(p + 1, t)
            score_rest(p, t, norms[p])

        send_edges(p)

    @pl.loop(0, inner)
    def _(i):
        for p in range(patches):
            score_plane(p, i, RIM + 1 + i - starts[p], *norms[p])

    shape = (prow, cols)
    count = jnp.full(shape, acq[0].astype(F32), F32)
    step = planes / jnp.maximum(count - 1.0, 1.0)
    anchor = jnp.full(shape, (me * planes).astype(F32), F32)
    last = (slabs * planes - 1) * 1.0
    for slot in range(MOST_ACQ):
        position = jnp.clip(anchor + (slot * step - 0.5), 0.0, last) - anchor
        for e in range(planes + 2):
            value = jnp.maximum(0.0, 1.0 - jnp.abs(position - (e - 1.0)))
            coef[slot, e] = jnp.where(count > slot, value, 0.0)

    for p in range(patches):

        @pl.when(has_right)
        def _():
            remote(snd_hi.at[p], rcv_below.at[p], edge, 2 * p, right).wait_send()
            remote(snd_lo.at[p], rcv_above.at[p], edge, 2 * p + 1, right).wait_recv()

        @pl.when(has_left)
        def _():
            remote(snd_lo.at[p], rcv_above.at[p], edge, 2 * p + 1, left).wait_send()
            remote(snd_hi.at[p], rcv_below.at[p], edge, 2 * p, left).wait_recv()

        def total(e, k):
            value = wpad[p, slot_of(p, e + RIM - 1), k]
            if e < EDGE:
                value = value + rcv_below[p, e, k]
            if e >= planes + 2 - EDGE:
                value = value + rcv_above[p, e - (planes + 2 - EDGE), k]
            return value

        inverses = [1.0 / (total(e, classes) + PRIOR) for e in range(planes + 2)]
        for k in range(classes):
            merged = []
            for e in range(planes + 2):
                value = total(e, k)
                if k == 0:
                    value = value + PRIOR
                merged.append(value * inverses[e])
            for slot in range(MOST_ACQ):
                value = coef[slot, 0] * merged[0]
                for e in range(1, planes + 2):
                    value = value + coef[slot, e] * merged[e]
                out[k, slot, p * prow : (p + 1) * prow, :] = value

    @pl.when(has_right)
    def _():
        halo_right.wait_send()

    @pl.when(has_left)
    def _():
        halo_left.wait_send()


def local(features, conv_weight, norm_gain, norm_bias, head_weight, head_bias, patch_offsets, fg_mask, acq_counts):
    channels, planes, rows, cols = features.shape
    folds, classes, _ = head_weight.shape
    patches = patch_offsets.shape[1]
    prow = rows // patches
    wide = folds * channels
    span = planes + 2 * RIM
    vmem = pl.BlockSpec(memory_space=pltpu.VMEM)
    smem = pl.BlockSpec(memory_space=pltpu.SMEM)
    edges = pltpu.VMEM((patches, EDGE, classes + 1, prow, cols), F32)
    cells = PATCH_X * prow * cols * patches
    return pl.pallas_call(
        kernel,
        out_shape=jax.ShapeDtypeStruct((classes, MOST_ACQ, rows, cols), F32),
        in_specs=[vmem] * 6 + [smem] * 3,
        out_specs=vmem,
        scratch_shapes=[
            pltpu.VMEM((channels, RIM, rows, cols), BF),
            pltpu.VMEM((channels, RIM, rows, cols), BF),
            pltpu.VMEM((patches, span + 2, (prow + 2) * 3 * channels, cols), BF),
            pltpu.VMEM((wide, 27 * channels), BF),
            pltpu.VMEM((patches, PATCH_X, wide, prow * cols), F32),
            pltpu.VMEM((patches, PATCH_X + 1, classes + 1, prow, cols), F32),
            edges, edges, edges, edges,
            pltpu.VMEM((patches, 3, wide, cols), F32),
            pltpu.VMEM((MOST_ACQ, planes + 2, prow, cols), F32),
            pltpu.SemaphoreType.DMA((2,)),
            pltpu.SemaphoreType.DMA((2,)),
            pltpu.SemaphoreType.DMA((2 * patches,)),
            pltpu.SemaphoreType.DMA((2 * patches,)),
        ],
        compiler_params=pltpu.CompilerParams(
            collective_id=0, has_side_effects=True, vmem_limit_bytes=30 * 1024 * 1024
        ),
        cost_estimate=pl.CostEstimate(
            flops=2 * cells * wide * 27 * channels,
            bytes_accessed=2 * features.size + 4 * classes * MOST_ACQ * rows * cols,
            transcendentals=cells * folds * classes,
        ),
    )(features, jnp.swapaxes(conv_weight, 1, 2), norm_gain, norm_bias, jnp.swapaxes(head_weight, 0, 1), head_bias, patch_offsets, fg_mask, acq_counts)


def solution(mesh):
    whole = P(None, ("brain", "slab"), None, None)
    by_slab = P(("brain", "slab"), None)
    in_specs = (whole, P(), P(), P(), P(), P(), by_slab, by_slab, P(("brain", "slab")))
    return jax.shard_map(local, mesh=mesh, in_specs=in_specs, out_specs=whole, check_vma=False)
```

```python
import functools

import jax
import jax.numpy as jnp
from jax import lax
from jax.experimental import pallas as pl
from jax.experimental.pallas import tpu as pltpu
from jax.sharding import PartitionSpec as P

MARGIN = 2
RIM = 4
PATCH_X = 10
MOST_ACQ = 8
PRIOR = 0.1
LEVELS = 65000
EDGE = RIM + 1
BF = jnp.bfloat16
F32 = jnp.float32


def iota(shape, dim):
    return lax.broadcasted_iota(jnp.int32, shape, dim)


def gauss(index, length):
    scaled = (index - (length - 1) / 2.0) / (length / 4.0)
    return jnp.exp(-0.5 * scaled * scaled)


def kernel(
    feat_in, wts_in, gain_in, bias_in, head_in, hbias_in, offs, keep_ref, acq,
    out,
    feat, wts, gain_ref, bias_ref, head_ref, hbias_ref,
    before, after, xs, wcat, conv, wpad, codes, snd_lo, snd_hi, rcv_below, rcv_above,
    meta_lo, meta_hi, meta_below, meta_above,
    stat, coef, load_sems, halo_send, halo_recv, edge_send, edge_recv,
):
    channels, planes, rows, cols = feat.shape
    classes, folds, _ = head_ref.shape
    patches = offs.shape[1]
    prow = rows // patches
    wide = folds * channels
    half = channels // 2
    slabs = lax.axis_size("slab")
    me = lax.axis_index("slab")
    has_left, has_right = me > 0, me < slabs - 1
    left, right = {"slab": me - 1}, {"slab": me + 1}

    loads = [
        pltpu.make_async_copy(src, dst, load_sems.at[i])
        for i, (src, dst) in enumerate(
            (
                (feat_in, feat), (wts_in, wts), (gain_in, gain_ref), (bias_in, bias_ref),
                (head_in, head_ref), (hbias_in, hbias_ref),
            )
        )
    ]
    for load in loads:
        load.start()

    barrier = pltpu.get_barrier_semaphore()

    @pl.when(has_left)
    def _():
        pl.semaphore_signal(barrier, inc=1, device_id=left)

    @pl.when(has_right)
    def _():
        pl.semaphore_signal(barrier, inc=1, device_id=right)

    interior = has_left & has_right

    @pl.when(interior)
    def _():
        pl.semaphore_wait(barrier, 2)

    @pl.when(jnp.logical_not(interior))
    def _():
        pl.semaphore_wait(barrier, 1)

    def remote(src, dst, sems, slot, target):
        return pltpu.make_async_remote_copy(
            src_ref=src, dst_ref=dst, send_sem=sems[0].at[slot], recv_sem=sems[1].at[slot],
            device_id=target,
        )

    halo = (halo_send, halo_recv)
    edge = (edge_send, edge_recv)
    halo_right = remote(feat_in.at[:, planes - RIM :], before, halo, 0, right)
    halo_left = remote(feat_in.at[:, :RIM], after, halo, 1, left)

    meta_right = remote(meta_hi, meta_below, halo, 2, right)
    meta_left = remote(meta_lo, meta_above, halo, 3, left)
    starts = [RIM - MARGIN + offs[0, p] for p in range(patches)]
    for p in range(patches):
        index = iota((8, cols), 0) - starts[p]
        keep = keep_ref[0, p].astype(F32)
        for ref, base in ((meta_lo, 0), (meta_hi, RIM + planes - 1)):
            i = index + base
            factor = gauss(i.astype(F32), PATCH_X) * keep
            ref[p] = jnp.where((i >= 0) & (i < PATCH_X), factor, 0.0)

    @pl.when(has_right)
    def _():
        halo_right.start()
        meta_right.start()

    @pl.when(has_left)
    def _():
        halo_left.start()
        meta_left.start()

    @pl.when(me == 0)
    def _():
        before[...] = jnp.zeros_like(before)
        rcv_below[...] = jnp.zeros_like(rcv_below)
        meta_below[...] = jnp.zeros_like(meta_below)

    @pl.when(me == slabs - 1)
    def _():
        after[...] = jnp.zeros_like(after)
        rcv_above[...] = jnp.zeros_like(rcv_above)
        meta_above[...] = jnp.zeros_like(meta_above)

    for load in loads[1:]:
        load.wait()

    inner = planes - 2
    rest = PATCH_X - inner

    depth = wts.shape[1]
    same = (iota((wide, wide), 0) == iota((wide, wide), 1)).astype(F32).astype(BF)
    wcat[...] = lax.dot_general(
        same, wts[...].reshape(3 * depth, wide), (((1,), (1,)), ((), ())), preferred_element_type=F32
    ).astype(BF)
    eye = iota((channels, channels), 0) == iota((channels, channels), 1)

    def column(values):
        return jnp.concatenate(
            [
                jnp.sum(jnp.where(eye, values[f : f + 1, :], 0.0), axis=1, keepdims=True)
                for f in range(folds)
            ],
            axis=0,
        )

    gain_col = column(gain_ref[...])
    bias_col = column(bias_ref[...])
    heads = folds * classes
    head_row = iota((heads, wide), 0)
    head_lane = iota((heads, wide), 1)
    flat_head = head_ref[...].astype(F32).reshape(heads, channels)
    head = jnp.concatenate([flat_head] * folds, axis=1)
    head = jnp.where(head_lane // channels == head_row % folds, head, 0.0)
    head2 = jnp.concatenate([head, head], axis=1).astype(BF)
    hb = jnp.concatenate([hbias_ref[...]] * classes, axis=0)
    pick = iota((heads, classes), 0) // folds == iota((heads, classes), 1)
    head_bias = jnp.sum(jnp.where(pick, hb, 0.0), axis=1, keepdims=True)

    m_i, k_i = iota((half * rows, half * rows), 0), iota((half * rows, half * rows), 1)
    swap = (k_i == (m_i % half) * rows + m_i // half).astype(F32).astype(BF)
    stack = heads * prow
    m_i, k_i = iota((classes * prow, stack), 0), iota((classes * prow, stack), 1)
    gather = (k_i // heads == m_i % prow) & ((k_i % heads) // folds == m_i // prow)
    gather = gather.astype(F32)
    gather = jnp.concatenate([gather, gather], axis=1).astype(BF)

    lane = iota((half * rows, cols), 1)
    unit = 3 * channels
    zero_row = jnp.zeros((unit, cols), BF)

    def lay_planes(source, first, base, count, masked):
        @pl.loop(0, count // 2)
        def _(pair):
            pair_planes = [source[:, first + 2 * pair + e].reshape(channels * rows, cols) for e in range(2)]
            for g in range(2):
                part = jnp.concatenate(
                    [v[g * half * rows : (g + 1) * half * rows] for v in pair_planes], axis=1
                )
                turned = jnp.dot(swap, part, preferred_element_type=F32)
                for e in range(2):
                    j = base + 2 * pair + e
                    here = turned[:, e * cols : (e + 1) * cols]
                    taps = (
                        jnp.where(lane == 0, 0.0, pltpu.roll(here, 1, 1)),
                        here,
                        jnp.where(lane == cols - 1, 0.0, pltpu.roll(here, cols - 1, 1)),
                    )
                    for p in range(patches):
                        if masked:
                            inside = (j >= starts[p]) & (j < starts[p] + PATCH_X)
                            factor = jnp.where(inside, 1.0, 0.0)
                        for c, tap in enumerate(taps):
                            mine = tap[p * prow * half : (p + 1) * prow * half]
                            if masked:
                                mine = mine * factor
                            mine = mine.astype(BF)
                            for r in range(prow):
                                at = (r + 1) * unit + c * channels + g * half
                                xs[p, j + 1, at : at + half, :] = mine[r * half : (r + 1) * half]

    span = planes + 2 * RIM
    for p in range(patches):
        xs[p, 0] = jnp.zeros((xs.shape[2], cols), BF)
        xs[p, span + 1] = jnp.zeros((xs.shape[2], cols), BF)

        @pl.loop(1, span + 1)
        def _(j, p=p):
            xs[p, j, 0:unit, :] = zero_row
            xs[p, j, (prow + 1) * unit : (prow + 2) * unit, :] = zero_row

        wpad[p, PATCH_X] = jnp.zeros(wpad.shape[2:], F32)
        codes[p, rest] = jnp.zeros(codes.shape[2:], codes.dtype)

    loads[0].wait()
    lay_planes(feat, 0, RIM, planes, False)

    def rest_index(p, t):
        return t + jnp.where(starts[p] + t <= RIM, 0, inner)

    def conv_plane(p, i, x):
        for pair in range(prow // 2):
            sides = []
            for h in (2 * pair, 2 * pair + 1):
                sides.append(
                    jnp.concatenate(
                        [xs[p, x + a, h * unit : h * unit + depth, :] for a in range(3)], axis=0
                    )
                )
            conv[p, i, :, 2 * pair * cols : (2 * pair + 2) * cols] = jnp.dot(
                wcat[...], jnp.concatenate(sides, axis=1), preferred_element_type=F32
            )

    def shift_of(p):
        total = conv[p, 0, :, 0:cols]
        for h in range(1, prow):
            total = total + conv[p, 0, :, h * cols : (h + 1) * cols]
        mean = jnp.sum(total, axis=1, keepdims=True) * (1.0 / (prow * cols))
        stat[p, 0] = jnp.broadcast_to(mean, (wide, cols))
        stat[p, 1] = jnp.zeros((wide, cols), F32)
        stat[p, 2] = jnp.zeros((wide, cols), F32)

    def add_stats(p, i):
        for lo in range(0, wide, 32):
            rows_here = slice(lo, lo + 32)
            base = stat[p, 0, rows_here]
            first, second = stat[p, 1, rows_here], stat[p, 2, rows_here]
            for h in range(prow):
                d = conv[p, i, rows_here, h * cols : (h + 1) * cols] - base
                first = first + d
                second = second + d * d
            stat[p, 1, rows_here] = first
            stat[p, 2, rows_here] = second

    def affine(p):
        size = 1.0 / (PATCH_X * prow * cols)
        d_mean = jnp.sum(stat[p, 1], axis=1, keepdims=True) * size
        var = jnp.sum(stat[p, 2], axis=1, keepdims=True) * size - d_mean * d_mean
        scale = lax.rsqrt(jnp.maximum(var, 0.0) + 1e-05) * gain_col
        mean = stat[p, 0][:, 0:1] + d_mean
        return scale, bias_col - mean * scale

    row_f = iota((prow, cols), 0).astype(F32)
    col_f = iota((prow, cols), 1).astype(F32)
    flat = gauss(row_f, prow) * gauss(col_f, cols)

    def score_plane(p, i, index, scale, offset, code=None):
        blocks = []
        for pair in range(prow // 2):
            y = conv[p, i, :, 2 * pair * cols : (2 * pair + 2) * cols] * scale + offset
            y = jnp.maximum(y, 0.01 * y)
            big = y.astype(BF)
            small = (y - big.astype(F32)).astype(BF)
            logits = jnp.dot(
                head2, jnp.concatenate([big, small], axis=0), preferred_element_type=F32
            ) + head_bias
            groups = [logits[j : j + 8] for j in range(0, heads, 8)]
            top = functools.reduce(jnp.maximum, groups)
            top = jnp.maximum(top, pltpu.roll(top, 4, 0))
            exps = [jnp.exp(v - top) for v in groups]
            total = functools.reduce(jnp.add, exps)
            total = total + pltpu.roll(total, 4, 0)
            inverse = 1.0 / total
            probs = jnp.concatenate([v * inverse for v in exps], axis=0)
            blocks += [probs[:, :cols], probs[:, cols:]]
        tall = jnp.concatenate(blocks, axis=0)
        big = tall.astype(BF)
        small = (tall - big.astype(F32)).astype(BF)
        summed = jnp.dot(
            gather, jnp.concatenate([big, small], axis=0), preferred_element_type=F32
        )
        index = lax.convert_element_type(index, F32)
        keep = keep_ref[0, p].astype(F32)
        window = gauss(jnp.full((prow, cols), index, F32), PATCH_X) * flat * keep
        share = window * (1.0 / folds)
        for k in range(classes):
            wpad[p, i, k] = summed[k * prow : (k + 1) * prow] * share
        wpad[p, i, classes] = window
        if code is not None:
            coded = (summed * (LEVELS / folds) + 0.5).astype(jnp.int32) - LEVELS // 2
            for k in range(classes // 2):
                codes[p, code, k] = coded[2 * k * prow : 2 * (k + 1) * prow].astype(jnp.int16)

    def slot_of(p, j):
        if RIM < j < RIM + planes - 1:
            return j - RIM - 1
        i = j - starts[p]
        if j <= RIM:
            return jnp.where(i >= 0, inner + i, PATCH_X)
        return jnp.where(i < PATCH_X, i, PATCH_X)

    def send_edges(p):
        for j in range(EDGE):
            snd_lo[p, j] = codes[p, slot_of(p, j) - inner]
            snd_hi[p, j] = codes[p, slot_of(p, RIM + planes - 1 + j) - inner]

        @pl.when(has_right)
        def _():
            remote(snd_hi.at[p], rcv_below.at[p], edge, 2 * p, right).start()

        @pl.when(has_left)
        def _():
            remote(snd_lo.at[p], rcv_above.at[p], edge, 2 * p + 1, left).start()

    for p in range(patches):
        conv_plane(p, 0, RIM + 1)
        shift_of(p)
        add_stats(p, 0)

        @pl.loop(1, inner)
        def _(i, p=p):
            conv_plane(p, i, RIM + 1 + i)
            add_stats(p, i)

    @pl.when(has_left)
    def _():
        remote(feat_in.at[:, planes - RIM :], before, halo, 0, left).wait_recv()
        remote(meta_hi, meta_below, halo, 2, left).wait_recv()

    @pl.when(has_right)
    def _():
        remote(feat_in.at[:, :RIM], after, halo, 1, right).wait_recv()
        remote(meta_lo, meta_above, halo, 3, right).wait_recv()

    lay_planes(before, 0, 0, RIM, True)
    lay_planes(after, 0, RIM + planes, RIM, True)

    def conv_rest(p, t):
        conv_plane(p, inner + t, starts[p] + rest_index(p, t))
        add_stats(p, inner + t)

    def score_rest(p, t, norms):
        score_plane(p, inner + t, rest_index(p, t), *norms, code=t)

    @pl.loop(0, rest)
    def _(t):
        conv_rest(0, t)

    norms = []
    for p in range(patches):
        norms.append(affine(p))

        @pl.loop(0, rest)
        def _(t, p=p):
            if p + 1 < patches:
                conv_rest(p + 1, t)
            score_rest(p, t, norms[p])

        send_edges(p)

    @pl.loop(0, inner)
    def _(i):
        for p in range(patches):
            score_plane(p, i, RIM + 1 + i - starts[p], *norms[p])

    shape = (prow, cols)
    count = jnp.full(shape, acq[0].astype(F32), F32)
    step = planes / jnp.maximum(count - 1.0, 1.0)
    anchor = jnp.full(shape, (me * planes).astype(F32), F32)
    last = (slabs * planes - 1) * 1.0
    for slot in range(MOST_ACQ):
        position = jnp.clip(anchor + (slot * step - 0.5), 0.0, last) - anchor
        for e in range(planes + 2):
            value = jnp.maximum(0.0, 1.0 - jnp.abs(position - (e - 1.0)))
            coef[slot, e] = jnp.where(count > slot, value, 0.0)

    for p in range(patches):

        @pl.when(has_right)
        def _():
            remote(snd_hi.at[p], rcv_below.at[p], edge, 2 * p, right).wait_send()
            remote(snd_lo.at[p], rcv_above.at[p], edge, 2 * p + 1, right).wait_recv()

        @pl.when(has_left)
        def _():
            remote(snd_lo.at[p], rcv_above.at[p], edge, 2 * p + 1, left).wait_send()
            remote(snd_hi.at[p], rcv_below.at[p], edge, 2 * p, left).wait_recv()

        ends = [(e, rcv_below, meta_below, e) for e in range(EDGE)]
        ends += [(planes + 2 - EDGE + j, rcv_above, meta_above, j) for j in range(EDGE)]

        def total(e, k):
            value = wpad[p, slot_of(p, e + RIM - 1), k]
            for plane, codes_in, meta, j in ends:
                if plane == e:
                    window = meta[p, j : j + 1, :] * flat
                    if k < classes:
                        half_at = (k % 2) * prow
                        got = codes_in[p, j, k // 2].astype(F32)[half_at : half_at + prow]
                        window = window * (got * (1.0 / LEVELS) + (LEVELS // 2) / LEVELS)
                    value = value + window
            return value

        inverses = [1.0 / (total(e, classes) + PRIOR) for e in range(planes + 2)]
        for k in range(classes):
            merged = []
            for e in range(planes + 2):
                value = total(e, k)
                if k == 0:
                    value = value + PRIOR
                merged.append(value * inverses[e])
            for slot in range(MOST_ACQ):
                value = coef[slot, 0] * merged[0]
                for e in range(1, planes + 2):
                    value = value + coef[slot, e] * merged[e]
                out[k, slot, p * prow : (p + 1) * prow, :] = value

    @pl.when(has_right)
    def _():
        halo_right.wait_send()
        meta_right.wait_send()

    @pl.when(has_left)
    def _():
        halo_left.wait_send()
        meta_left.wait_send()


def local(features, conv_weight, norm_gain, norm_bias, head_weight, head_bias, patch_offsets, fg_mask, acq_counts):
    channels, planes, rows, cols = features.shape
    folds, classes, _ = head_weight.shape
    patches = patch_offsets.shape[1]
    prow = rows // patches
    wide = folds * channels
    span = planes + 2 * RIM
    vmem = pl.BlockSpec(memory_space=pltpu.VMEM)
    smem = pl.BlockSpec(memory_space=pltpu.SMEM)
    hbm = pl.BlockSpec(memory_space=pltpu.MemorySpace.HBM)
    edges = pltpu.VMEM((patches, EDGE, classes // 2, 2 * prow, cols), jnp.int16)
    meta = pltpu.VMEM((patches, 8, cols), F32)
    rest = PATCH_X - (planes - 2)
    operands = (
        features, jnp.swapaxes(conv_weight, 1, 2), norm_gain, norm_bias,
        jnp.swapaxes(head_weight, 0, 1), head_bias,
    )
    cells = PATCH_X * prow * cols * patches
    return pl.pallas_call(
        kernel,
        out_shape=jax.ShapeDtypeStruct((classes, MOST_ACQ, rows, cols), F32),
        in_specs=[hbm] * 6 + [smem] * 3,
        out_specs=vmem,
        scratch_shapes=[
            *[pltpu.VMEM(value.shape, value.dtype) for value in operands],
            pltpu.VMEM((channels, RIM, rows, cols), BF),
            pltpu.VMEM((channels, RIM, rows, cols), BF),
            pltpu.VMEM((patches, span + 2, (prow + 2) * 3 * channels, cols), BF),
            pltpu.VMEM((wide, 27 * channels), BF),
            pltpu.VMEM((patches, PATCH_X, wide, prow * cols), F32),
            pltpu.VMEM((patches, PATCH_X + 1, classes + 1, prow, cols), F32),
            pltpu.VMEM((patches, rest + 1, classes // 2, 2 * prow, cols), jnp.int16),
            edges, edges, edges, edges,
            meta, meta, meta, meta,
            pltpu.VMEM((patches, 3, wide, cols), F32),
            pltpu.VMEM((MOST_ACQ, planes + 2, prow, cols), F32),
            pltpu.SemaphoreType.DMA((6,)),
            pltpu.SemaphoreType.DMA((4,)),
            pltpu.SemaphoreType.DMA((4,)),
            pltpu.SemaphoreType.DMA((2 * patches,)),
            pltpu.SemaphoreType.DMA((2 * patches,)),
        ],
        compiler_params=pltpu.CompilerParams(
            collective_id=0, has_side_effects=True, vmem_limit_bytes=56 * 1024 * 1024
        ),
        cost_estimate=pl.CostEstimate(
            flops=2 * cells * wide * 27 * channels,
            bytes_accessed=2 * features.size + 4 * classes * MOST_ACQ * rows * cols,
            transcendentals=cells * folds * classes,
        ),
    )(*operands, patch_offsets, fg_mask, acq_counts)


def solution(mesh):
    whole = P(None, ("brain", "slab"), None, None)
    by_slab = P(("brain", "slab"), None)
    in_specs = (whole, P(), P(), P(), P(), P(), by_slab, by_slab, P(("brain", "slab")))
    return jax.shard_map(local, mesh=mesh, in_specs=in_specs, out_specs=whole, check_vma=False)
```

```python
import functools

import jax
import jax.numpy as jnp
from jax import lax
from jax.experimental import pallas as pl
from jax.experimental.pallas import tpu as pltpu
from jax.sharding import PartitionSpec as P

MARGIN = 2
RIM = 4
PATCH_X = 10
MOST_ACQ = 8
PRIOR = 0.1
LEVELS = 65000
EDGE = RIM + 1
BF = jnp.bfloat16
F32 = jnp.float32


def iota(shape, dim):
    return lax.broadcasted_iota(jnp.int32, shape, dim)


def gauss(index, length):
    scaled = (index - (length - 1) / 2.0) / (length / 4.0)
    return jnp.exp(-0.5 * scaled * scaled)


def kernel(
    feat_in, wts_in, gain_in, bias_in, head_in, hbias_in, offs, keep_ref, acq,
    out,
    feat, wts, gain_ref, bias_ref, head_ref, hbias_ref,
    before, after, xs, wcat, conv, wpad, codes, snd_lo, snd_hi, rcv_below, rcv_above,
    meta_lo, meta_hi, meta_below, meta_above,
    stat, coef, load_sems, halo_send, halo_recv, edge_send, edge_recv,
):
    channels, planes, rows, cols = feat.shape
    classes, folds, _ = head_ref.shape
    patches = offs.shape[1]
    prow = rows // patches
    wide = folds * channels
    half = channels // 2
    slabs = lax.axis_size("slab")
    me = lax.axis_index("slab")
    has_left, has_right = me > 0, me < slabs - 1
    left, right = {"slab": me - 1}, {"slab": me + 1}

    loads = [
        pltpu.make_async_copy(src, dst, load_sems.at[i])
        for i, (src, dst) in enumerate(
            (
                (feat_in, feat), (wts_in, wts), (gain_in, gain_ref), (bias_in, bias_ref),
                (head_in, head_ref), (hbias_in, hbias_ref),
            )
        )
    ]
    for load in loads:
        load.start()

    barrier = pltpu.get_barrier_semaphore()

    @pl.when(has_left)
    def _():
        pl.semaphore_signal(barrier, inc=1, device_id=left)

    @pl.when(has_right)
    def _():
        pl.semaphore_signal(barrier, inc=1, device_id=right)

    interior = has_left & has_right

    @pl.when(interior)
    def _():
        pl.semaphore_wait(barrier, 2)

    @pl.when(jnp.logical_not(interior))
    def _():
        pl.semaphore_wait(barrier, 1)

    def remote(src, dst, sems, slot, target):
        return pltpu.make_async_remote_copy(
            src_ref=src, dst_ref=dst, send_sem=sems[0].at[slot], recv_sem=sems[1].at[slot],
            device_id=target,
        )

    halo = (halo_send, halo_recv)
    edge = (edge_send, edge_recv)
    halo_right = remote(feat_in.at[:, planes - RIM :], before, halo, 0, right)
    halo_left = remote(feat_in.at[:, :RIM], after, halo, 1, left)

    meta_right = remote(meta_hi, meta_below, halo, 2, right)
    meta_left = remote(meta_lo, meta_above, halo, 3, left)
    starts = [RIM - MARGIN + offs[0, p] for p in range(patches)]
    for p in range(patches):
        index = iota((8, cols), 0) - starts[p]
        keep = keep_ref[0, p].astype(F32)
        for ref, base in ((meta_lo, 0), (meta_hi, RIM + planes - 1)):
            i = index + base
            factor = gauss(i.astype(F32), PATCH_X) * keep
            ref[p] = jnp.where((i >= 0) & (i < PATCH_X), factor, 0.0)

    @pl.when(has_right)
    def _():
        halo_right.start()
        meta_right.start()

    @pl.when(has_left)
    def _():
        halo_left.start()
        meta_left.start()

    @pl.when(me == 0)
    def _():
        before[...] = jnp.zeros_like(before)
        rcv_below[...] = jnp.zeros_like(rcv_below)
        meta_below[...] = jnp.zeros_like(meta_below)

    @pl.when(me == slabs - 1)
    def _():
        after[...] = jnp.zeros_like(after)
        rcv_above[...] = jnp.zeros_like(rcv_above)
        meta_above[...] = jnp.zeros_like(meta_above)

    for load in loads[1:]:
        load.wait()

    inner = planes - 2
    rest = PATCH_X - inner

    depth = wts.shape[1]
    same = (iota((wide, wide), 0) == iota((wide, wide), 1)).astype(F32).astype(BF)
    wcat[...] = lax.dot_general(
        same, wts[...].reshape(3 * depth, wide), (((1,), (1,)), ((), ())), preferred_element_type=F32
    ).astype(BF)
    eye = iota((channels, channels), 0) == iota((channels, channels), 1)

    def column(values):
        return jnp.concatenate(
            [
                jnp.sum(jnp.where(eye, values[f : f + 1, :], 0.0), axis=1, keepdims=True)
                for f in range(folds)
            ],
            axis=0,
        )

    gain_col = column(gain_ref[...])
    bias_col = column(bias_ref[...])
    heads = folds * classes
    head_row = iota((heads, wide), 0)
    head_lane = iota((heads, wide), 1)
    flat_head = head_ref[...].astype(F32).reshape(heads, channels)
    head = jnp.concatenate([flat_head] * folds, axis=1)
    head = jnp.where(head_lane // channels == head_row % folds, head, 0.0)
    head2 = jnp.concatenate([head, head], axis=1).astype(BF)
    hb = jnp.concatenate([hbias_ref[...]] * classes, axis=0)
    pick = iota((heads, classes), 0) // folds == iota((heads, classes), 1)
    head_bias = jnp.sum(jnp.where(pick, hb, 0.0), axis=1, keepdims=True)

    m_i, k_i = iota((half * rows, half * rows), 0), iota((half * rows, half * rows), 1)
    swap = (k_i == (m_i % half) * rows + m_i // half).astype(F32).astype(BF)
    stack = heads * prow
    m_i, k_i = iota((classes * prow, stack), 0), iota((classes * prow, stack), 1)
    gather = (k_i // heads == m_i % prow) & ((k_i % heads) // folds == m_i // prow)
    gather = gather.astype(F32)
    gather = jnp.concatenate([gather, gather], axis=1).astype(BF)

    lane = iota((half * rows, cols), 1)
    unit = 3 * channels
    zero_row = jnp.zeros((unit, cols), BF)

    def lay_planes(source, first, base, count, masked):
        @pl.loop(0, count // 2)
        def _(pair):
            pair_planes = [source[:, first + 2 * pair + e].reshape(channels * rows, cols) for e in range(2)]
            for g in range(2):
                part = jnp.concatenate(
                    [v[g * half * rows : (g + 1) * half * rows] for v in pair_planes], axis=1
                )
                turned = jnp.dot(swap, part, preferred_element_type=F32)
                for e in range(2):
                    j = base + 2 * pair + e
                    here = turned[:, e * cols : (e + 1) * cols]
                    taps = (
                        jnp.where(lane == 0, 0.0, pltpu.roll(here, 1, 1)),
                        here,
                        jnp.where(lane == cols - 1, 0.0, pltpu.roll(here, cols - 1, 1)),
                    )
                    for p in range(patches):
                        if masked:
                            inside = (j >= starts[p]) & (j < starts[p] + PATCH_X)
                            factor = jnp.where(inside, 1.0, 0.0)
                        for c, tap in enumerate(taps):
                            mine = tap[p * prow * half : (p + 1) * prow * half]
                            if masked:
                                mine = mine * factor
                            mine = mine.astype(BF)
                            for r in range(prow):
                                at = (r + 1) * unit + c * channels + g * half
                                xs[p, j + 1, at : at + half, :] = mine[r * half : (r + 1) * half]

    span = planes + 2 * RIM
    for p in range(patches):
        xs[p, 0] = jnp.zeros((xs.shape[2], cols), BF)
        xs[p, span + 1] = jnp.zeros((xs.shape[2], cols), BF)

        @pl.loop(1, span + 1)
        def _(j, p=p):
            xs[p, j, 0:unit, :] = zero_row
            xs[p, j, (prow + 1) * unit : (prow + 2) * unit, :] = zero_row

        wpad[p, PATCH_X] = jnp.zeros(wpad.shape[2:], F32)
        codes[p, rest] = jnp.zeros(codes.shape[2:], codes.dtype)

    loads[0].wait()
    lay_planes(feat, 0, RIM, planes, False)

    def rest_index(p, t):
        return t + jnp.where(starts[p] + t <= RIM, 0, inner)

    def conv_plane(p, i, x):
        for pair in range(prow // 2):
            sides = []
            for h in (2 * pair, 2 * pair + 1):
                sides.append(
                    jnp.concatenate(
                        [xs[p, x + a, h * unit : h * unit + depth, :] for a in range(3)], axis=0
                    )
                )
            conv[p, i, :, 2 * pair * cols : (2 * pair + 2) * cols] = jnp.dot(
                wcat[...], jnp.concatenate(sides, axis=1), preferred_element_type=F32
            )

    def shift_of(p):
        total = conv[p, 0, :, 0:cols]
        for h in range(1, prow):
            total = total + conv[p, 0, :, h * cols : (h + 1) * cols]
        mean = jnp.sum(total, axis=1, keepdims=True) * (1.0 / (prow * cols))
        stat[p, 0] = jnp.broadcast_to(mean, (wide, cols))
        stat[p, 1] = jnp.zeros((wide, cols), F32)
        stat[p, 2] = jnp.zeros((wide, cols), F32)

    def add_stats(p, i):
        for lo in range(0, wide, 32):
            rows_here = slice(lo, lo + 32)
            base = stat[p, 0, rows_here]
            first, second = stat[p, 1, rows_here], stat[p, 2, rows_here]
            for h in range(prow):
                d = conv[p, i, rows_here, h * cols : (h + 1) * cols] - base
                first = first + d
                second = second + d * d
            stat[p, 1, rows_here] = first
            stat[p, 2, rows_here] = second

    def affine(p):
        size = 1.0 / (PATCH_X * prow * cols)
        d_mean = jnp.sum(stat[p, 1], axis=1, keepdims=True) * size
        var = jnp.sum(stat[p, 2], axis=1, keepdims=True) * size - d_mean * d_mean
        scale = lax.rsqrt(jnp.maximum(var, 0.0) + 1e-05) * gain_col
        mean = stat[p, 0][:, 0:1] + d_mean
        return scale, bias_col - mean * scale

    row_f = iota((prow, cols), 0).astype(F32)
    col_f = iota((prow, cols), 1).astype(F32)
    flat = gauss(row_f, prow) * gauss(col_f, cols)

    def score_plane(p, i, index, scale, offset, code=None):
        blocks = []
        for pair in range(prow // 2):
            y = conv[p, i, :, 2 * pair * cols : (2 * pair + 2) * cols] * scale + offset
            y = jnp.maximum(y, 0.01 * y)
            big = y.astype(BF)
            small = (y - big.astype(F32)).astype(BF)
            logits = jnp.dot(
                head2, jnp.concatenate([big, small], axis=0), preferred_element_type=F32
            ) + head_bias
            groups = [logits[j : j + 8] for j in range(0, heads, 8)]
            top = functools.reduce(jnp.maximum, groups)
            top = jnp.maximum(top, pltpu.roll(top, 4, 0))
            exps = [jnp.exp(v - top) for v in groups]
            total = functools.reduce(jnp.add, exps)
            total = total + pltpu.roll(total, 4, 0)
            inverse = 1.0 / total
            probs = jnp.concatenate([v * inverse for v in exps], axis=0)
            blocks += [probs[:, :cols], probs[:, cols:]]
        tall = jnp.concatenate(blocks, axis=0)
        big = tall.astype(BF)
        small = (tall - big.astype(F32)).astype(BF)
        summed = jnp.dot(
            gather, jnp.concatenate([big, small], axis=0), preferred_element_type=F32
        )
        index = lax.convert_element_type(index, F32)
        keep = keep_ref[0, p].astype(F32)
        window = gauss(jnp.full((prow, cols), index, F32), PATCH_X) * flat * keep
        share = window * (1.0 / folds)
        for k in range(classes):
            wpad[p, i, k] = summed[k * prow : (k + 1) * prow] * share
        wpad[p, i, classes] = window
        if code is not None:
            coded = (summed * (LEVELS / folds) + 0.5).astype(jnp.int32) - LEVELS // 2
            for k in range(classes // 2):
                codes[p, code, k] = coded[2 * k * prow : 2 * (k + 1) * prow].astype(jnp.int16)

    def slot_of(p, j):
        if RIM < j < RIM + planes - 1:
            return j - RIM - 1
        i = j - starts[p]
        if j <= RIM:
            return jnp.where(i >= 0, inner + i, PATCH_X)
        return jnp.where(i < PATCH_X, i, PATCH_X)

    def send_edges(p):
        for j in range(EDGE):
            snd_lo[p, j] = codes[p, slot_of(p, j) - inner]
            snd_hi[p, j] = codes[p, slot_of(p, RIM + planes - 1 + j) - inner]

        @pl.when(has_right)
        def _():
            remote(snd_hi.at[p], rcv_below.at[p], edge, 2 * p, right).start()

        @pl.when(has_left)
        def _():
            remote(snd_lo.at[p], rcv_above.at[p], edge, 2 * p + 1, left).start()

    shape = (prow, cols)
    count = jnp.full(shape, acq[0].astype(F32), F32)
    step = planes / jnp.maximum(count - 1.0, 1.0)
    anchor = jnp.full(shape, (me * planes).astype(F32), F32)
    last = (slabs * planes - 1) * 1.0
    for slot in range(MOST_ACQ):
        position = jnp.clip(anchor + (slot * step - 0.5), 0.0, last) - anchor
        for e in range(planes + 2):
            value = jnp.maximum(0.0, 1.0 - jnp.abs(position - (e - 1.0)))
            coef[slot, e] = jnp.where(count > slot, value, 0.0)

    for p in range(patches):
        conv_plane(p, 0, RIM + 1)
        shift_of(p)
        add_stats(p, 0)

    @pl.loop(1, inner)
    def _(i):
        for p in range(patches):
            conv_plane(p, i, RIM + 1 + i)
            add_stats(p, i)

    @pl.when(has_left)
    def _():
        remote(feat_in.at[:, planes - RIM :], before, halo, 0, left).wait_recv()
        remote(meta_hi, meta_below, halo, 2, left).wait_recv()

    @pl.when(has_right)
    def _():
        remote(feat_in.at[:, :RIM], after, halo, 1, right).wait_recv()
        remote(meta_lo, meta_above, halo, 3, right).wait_recv()

    lay_planes(before, 0, 0, RIM, True)
    lay_planes(after, 0, RIM + planes, RIM, True)

    def conv_rest(p, t):
        conv_plane(p, inner + t, starts[p] + rest_index(p, t))
        add_stats(p, inner + t)

    def score_rest(p, t, norms):
        score_plane(p, inner + t, rest_index(p, t), *norms, code=t)

    @pl.loop(0, rest)
    def _(t):
        conv_rest(0, t)

    norms = []
    for p in range(patches):
        norms.append(affine(p))

        if p + 1 < patches:

            @pl.loop(0, rest)
            def _(t, p=p):
                conv_rest(p + 1, t)
                score_rest(p, t, norms[p])
        else:

            @pl.loop(0, rest // 2)
            def _(t, p=p):
                score_rest(p, 2 * t, norms[p])
                score_rest(p, 2 * t + 1, norms[p])
            if rest % 2:
                score_rest(p, rest - 1, norms[p])

        send_edges(p)

    @pl.loop(0, inner)
    def _(i):
        for p in range(patches):
            score_plane(p, i, RIM + 1 + i - starts[p], *norms[p])

    for p in range(patches):

        @pl.when(has_right)
        def _():
            remote(snd_hi.at[p], rcv_below.at[p], edge, 2 * p, right).wait_send()
            remote(snd_lo.at[p], rcv_above.at[p], edge, 2 * p + 1, right).wait_recv()

        @pl.when(has_left)
        def _():
            remote(snd_lo.at[p], rcv_above.at[p], edge, 2 * p + 1, left).wait_send()
            remote(snd_hi.at[p], rcv_below.at[p], edge, 2 * p, left).wait_recv()

        ends = [(e, rcv_below, meta_below, e) for e in range(EDGE)]
        ends += [(planes + 2 - EDGE + j, rcv_above, meta_above, j) for j in range(EDGE)]

        def total(e, k):
            value = wpad[p, slot_of(p, e + RIM - 1), k]
            for plane, codes_in, meta, j in ends:
                if plane == e:
                    window = meta[p, j : j + 1, :] * flat
                    if k < classes:
                        half_at = (k % 2) * prow
                        got = codes_in[p, j, k // 2].astype(F32)[half_at : half_at + prow]
                        window = window * (got * (1.0 / LEVELS) + (LEVELS // 2) / LEVELS)
                    value = value + window
            return value

        inverses = [1.0 / (total(e, classes) + PRIOR) for e in range(planes + 2)]
        for k in range(classes):
            merged = []
            for e in range(planes + 2):
                value = total(e, k)
                if k == 0:
                    value = value + PRIOR
                merged.append(value * inverses[e])
            for slot in range(MOST_ACQ):
                value = coef[slot, 0] * merged[0]
                for e in range(1, planes + 2):
                    value = value + coef[slot, e] * merged[e]
                out[k, slot, p * prow : (p + 1) * prow, :] = value

    @pl.when(has_right)
    def _():
        halo_right.wait_send()
        meta_right.wait_send()

    @pl.when(has_left)
    def _():
        halo_left.wait_send()
        meta_left.wait_send()


def local(features, conv_weight, norm_gain, norm_bias, head_weight, head_bias, patch_offsets, fg_mask, acq_counts):
    channels, planes, rows, cols = features.shape
    folds, classes, _ = head_weight.shape
    patches = patch_offsets.shape[1]
    prow = rows // patches
    wide = folds * channels
    span = planes + 2 * RIM
    vmem = pl.BlockSpec(memory_space=pltpu.VMEM)
    smem = pl.BlockSpec(memory_space=pltpu.SMEM)
    hbm = pl.BlockSpec(memory_space=pltpu.MemorySpace.HBM)
    edges = pltpu.VMEM((patches, EDGE, classes // 2, 2 * prow, cols), jnp.int16)
    meta = pltpu.VMEM((patches, 8, cols), F32)
    rest = PATCH_X - (planes - 2)
    operands = (
        features, jnp.swapaxes(conv_weight, 1, 2), norm_gain, norm_bias,
        jnp.swapaxes(head_weight, 0, 1), head_bias,
    )
    cells = PATCH_X * prow * cols * patches
    return pl.pallas_call(
        kernel,
        out_shape=jax.ShapeDtypeStruct((classes, MOST_ACQ, rows, cols), F32),
        in_specs=[hbm] * 6 + [smem] * 3,
        out_specs=vmem,
        scratch_shapes=[
            *[pltpu.VMEM(value.shape, value.dtype) for value in operands],
            pltpu.VMEM((channels, RIM, rows, cols), BF),
            pltpu.VMEM((channels, RIM, rows, cols), BF),
            pltpu.VMEM((patches, span + 2, (prow + 2) * 3 * channels, cols), BF),
            pltpu.VMEM((wide, 27 * channels), BF),
            pltpu.VMEM((patches, PATCH_X, wide, prow * cols), F32),
            pltpu.VMEM((patches, PATCH_X + 1, classes + 1, prow, cols), F32),
            pltpu.VMEM((patches, rest + 1, classes // 2, 2 * prow, cols), jnp.int16),
            edges, edges, edges, edges,
            meta, meta, meta, meta,
            pltpu.VMEM((patches, 3, wide, cols), F32),
            pltpu.VMEM((MOST_ACQ, planes + 2, prow, cols), F32),
            pltpu.SemaphoreType.DMA((6,)),
            pltpu.SemaphoreType.DMA((4,)),
            pltpu.SemaphoreType.DMA((4,)),
            pltpu.SemaphoreType.DMA((2 * patches,)),
            pltpu.SemaphoreType.DMA((2 * patches,)),
        ],
        compiler_params=pltpu.CompilerParams(
            collective_id=0, has_side_effects=True, vmem_limit_bytes=56 * 1024 * 1024
        ),
        cost_estimate=pl.CostEstimate(
            flops=2 * cells * wide * 27 * channels,
            bytes_accessed=2 * features.size + 4 * classes * MOST_ACQ * rows * cols,
            transcendentals=cells * folds * classes,
        ),
    )(*operands, patch_offsets, fg_mask, acq_counts)


def solution(mesh):
    whole = P(None, ("brain", "slab"), None, None)
    by_slab = P(("brain", "slab"), None)
    in_specs = (whole, P(), P(), P(), P(), P(), by_slab, by_slab, P(("brain", "slab")))
    return jax.shard_map(local, mesh=mesh, in_specs=in_specs, out_specs=whole, check_vma=False)
```

```python
import functools

import jax
import jax.numpy as jnp
from jax import lax
from jax.experimental import pallas as pl
from jax.experimental.pallas import tpu as pltpu
from jax.sharding import PartitionSpec as P

MARGIN = 2
RIM = 4
PATCH_X = 10
MOST_ACQ = 8
PRIOR = 0.1
LEVELS = 65000
EDGE = RIM + 1
BF = jnp.bfloat16
F32 = jnp.float32


def iota(shape, dim):
    return lax.broadcasted_iota(jnp.int32, shape, dim)


def gauss(index, length):
    scaled = (index - (length - 1) / 2.0) / (length / 4.0)
    return jnp.exp(-0.5 * scaled * scaled)


def kernel(
    feat_in, wts_in, gain_in, bias_in, head_in, hbias_in, offs, keep_ref, acq,
    out,
    feat, wts, gain_ref, bias_ref, head_ref, hbias_ref,
    before, after, xs, wcat, conv, wpad, codes, snd_lo, snd_hi, rcv_below, rcv_above,
    meta_lo, meta_hi, meta_below, meta_above,
    stat, coef, load_sems, halo_send, halo_recv, edge_send, edge_recv,
):
    channels, planes, rows, cols = feat.shape
    classes, folds, _ = head_ref.shape
    patches = offs.shape[1]
    prow = rows // patches
    wide = folds * channels
    half = channels // 2
    slabs = lax.axis_size("slab")
    me = lax.axis_index("slab")
    has_left, has_right = me > 0, me < slabs - 1
    left, right = {"slab": me - 1}, {"slab": me + 1}

    loads = [
        pltpu.make_async_copy(src, dst, load_sems.at[i])
        for i, (src, dst) in enumerate(
            (
                (feat_in, feat), (wts_in, wts), (gain_in, gain_ref), (bias_in, bias_ref),
                (head_in, head_ref), (hbias_in, hbias_ref),
            )
        )
    ]
    for load in loads:
        load.start()

    barrier = pltpu.get_barrier_semaphore()

    @pl.when(has_left)
    def _():
        pl.semaphore_signal(barrier, inc=1, device_id=left)

    @pl.when(has_right)
    def _():
        pl.semaphore_signal(barrier, inc=1, device_id=right)

    interior = has_left & has_right

    @pl.when(interior)
    def _():
        pl.semaphore_wait(barrier, 2)

    @pl.when(jnp.logical_not(interior))
    def _():
        pl.semaphore_wait(barrier, 1)

    def remote(src, dst, sems, slot, target):
        return pltpu.make_async_remote_copy(
            src_ref=src, dst_ref=dst, send_sem=sems[0].at[slot], recv_sem=sems[1].at[slot],
            device_id=target,
        )

    halo = (halo_send, halo_recv)
    edge = (edge_send, edge_recv)
    halo_right = remote(feat_in.at[:, planes - RIM :], before, halo, 0, right)
    halo_left = remote(feat_in.at[:, :RIM], after, halo, 1, left)

    meta_right = remote(meta_hi, meta_below, halo, 2, right)
    meta_left = remote(meta_lo, meta_above, halo, 3, left)
    starts = [RIM - MARGIN + offs[0, p] for p in range(patches)]
    for p in range(patches):
        index = iota((8, cols), 0) - starts[p]
        keep = keep_ref[0, p].astype(F32)
        for ref, base in ((meta_lo, 0), (meta_hi, RIM + planes - 1)):
            i = index + base
            factor = gauss(i.astype(F32), PATCH_X) * keep
            ref[p] = jnp.where((i >= 0) & (i < PATCH_X), factor, 0.0)

    @pl.when(has_right)
    def _():
        halo_right.start()
        meta_right.start()

    @pl.when(has_left)
    def _():
        halo_left.start()
        meta_left.start()

    @pl.when(me == 0)
    def _():
        before[...] = jnp.zeros_like(before)
        rcv_below[...] = jnp.zeros_like(rcv_below)
        meta_below[...] = jnp.zeros_like(meta_below)

    @pl.when(me == slabs - 1)
    def _():
        after[...] = jnp.zeros_like(after)
        rcv_above[...] = jnp.zeros_like(rcv_above)
        meta_above[...] = jnp.zeros_like(meta_above)

    for load in loads[1:]:
        load.wait()

    inner = planes - 2
    rest = PATCH_X - inner

    depth = wts.shape[1]
    same = (iota((wide, wide), 0) == iota((wide, wide), 1)).astype(F32).astype(BF)
    wcat[...] = lax.dot_general(
        same, wts[...].reshape(3 * depth, wide), (((1,), (1,)), ((), ())), preferred_element_type=F32
    ).astype(BF)
    eye = iota((channels, channels), 0) == iota((channels, channels), 1)

    def column(values):
        return jnp.concatenate(
            [
                jnp.sum(jnp.where(eye, values[f : f + 1, :], 0.0), axis=1, keepdims=True)
                for f in range(folds)
            ],
            axis=0,
        )

    gain_col = column(gain_ref[...])
    bias_col = column(bias_ref[...])
    heads = folds * classes
    head_row = iota((heads, wide), 0)
    head_lane = iota((heads, wide), 1)
    flat_head = head_ref[...].astype(F32).reshape(heads, channels)
    head = jnp.concatenate([flat_head] * folds, axis=1)
    head = jnp.where(head_lane // channels == head_row % folds, head, 0.0)
    head2 = jnp.concatenate([head, head], axis=1).astype(BF)
    hb = jnp.concatenate([hbias_ref[...]] * classes, axis=0)
    pick = iota((heads, classes), 0) // folds == iota((heads, classes), 1)
    head_bias = jnp.sum(jnp.where(pick, hb, 0.0), axis=1, keepdims=True)

    m_i, k_i = iota((half * rows, half * rows), 0), iota((half * rows, half * rows), 1)
    swap = (k_i == (m_i % half) * rows + m_i // half).astype(F32).astype(BF)
    stack = heads * prow
    m_i, k_i = iota((classes * prow, stack), 0), iota((classes * prow, stack), 1)
    gather = (k_i // heads == m_i % prow) & ((k_i % heads) // folds == m_i // prow)
    gather = gather.astype(F32)
    gather = jnp.concatenate([gather, gather], axis=1).astype(BF)

    lane = iota((half * rows, cols), 1)
    unit = 3 * channels
    zero_row = jnp.zeros((unit, cols), BF)

    def lay_planes(source, first, base, count, masked):
        @pl.loop(0, count // 2)
        def _(pair):
            pair_planes = [source[:, first + 2 * pair + e].reshape(channels * rows, cols) for e in range(2)]
            for g in range(2):
                part = jnp.concatenate(
                    [v[g * half * rows : (g + 1) * half * rows] for v in pair_planes], axis=1
                )
                turned = jnp.dot(swap, part, preferred_element_type=F32)
                for e in range(2):
                    j = base + 2 * pair + e
                    here = turned[:, e * cols : (e + 1) * cols]
                    taps = (
                        jnp.where(lane == 0, 0.0, pltpu.roll(here, 1, 1)),
                        here,
                        jnp.where(lane == cols - 1, 0.0, pltpu.roll(here, cols - 1, 1)),
                    )
                    for p in range(patches):
                        if masked:
                            inside = (j >= starts[p]) & (j < starts[p] + PATCH_X)
                            factor = jnp.where(inside, 1.0, 0.0)
                        for c, tap in enumerate(taps):
                            mine = tap[p * prow * half : (p + 1) * prow * half]
                            if masked:
                                mine = mine * factor
                            mine = mine.astype(BF)
                            for r in range(prow):
                                at = (r + 1) * unit + c * channels + g * half
                                xs[p, j + 1, at : at + half, :] = mine[r * half : (r + 1) * half]

    span = planes + 2 * RIM
    for p in range(patches):
        xs[p, 0] = jnp.zeros((xs.shape[2], cols), BF)
        xs[p, span + 1] = jnp.zeros((xs.shape[2], cols), BF)

        @pl.loop(1, span + 1)
        def _(j, p=p):
            xs[p, j, 0:unit, :] = zero_row
            xs[p, j, (prow + 1) * unit : (prow + 2) * unit, :] = zero_row

        wpad[p, PATCH_X] = jnp.zeros(wpad.shape[2:], F32)
        codes[p, rest] = jnp.zeros(codes.shape[2:], codes.dtype)

    loads[0].wait()
    lay_planes(feat, 0, RIM, planes, False)

    def rest_index(p, t):
        return t + jnp.where(starts[p] + t <= RIM, 0, inner)

    def conv_plane(p, i, x):
        for pair in range(prow // 2):
            sides = []
            for h in (2 * pair, 2 * pair + 1):
                sides.append(
                    jnp.concatenate(
                        [xs[p, x + a, h * unit : h * unit + depth, :] for a in range(3)], axis=0
                    )
                )
            conv[p, i, :, 2 * pair * cols : (2 * pair + 2) * cols] = jnp.dot(
                wcat[...], jnp.concatenate(sides, axis=1), preferred_element_type=F32
            )

    def shift_of(p):
        total = conv[p, 0, :, 0:cols]
        for h in range(1, prow):
            total = total + conv[p, 0, :, h * cols : (h + 1) * cols]
        mean = jnp.sum(total, axis=1, keepdims=True) * (1.0 / (prow * cols))
        stat[p, 0] = jnp.broadcast_to(mean, (wide, cols))
        stat[p, 1] = jnp.zeros((wide, cols), F32)
        stat[p, 2] = jnp.zeros((wide, cols), F32)

    def add_stats(p, i):
        for lo in range(0, wide, 32):
            rows_here = slice(lo, lo + 32)
            base = stat[p, 0, rows_here]
            first, second = stat[p, 1, rows_here], stat[p, 2, rows_here]
            for h in range(prow):
                d = conv[p, i, rows_here, h * cols : (h + 1) * cols] - base
                first = first + d
                second = second + d * d
            stat[p, 1, rows_here] = first
            stat[p, 2, rows_here] = second

    def affine(p):
        size = 1.0 / (PATCH_X * prow * cols)
        d_mean = jnp.sum(stat[p, 1], axis=1, keepdims=True) * size
        var = jnp.sum(stat[p, 2], axis=1, keepdims=True) * size - d_mean * d_mean
        scale = lax.rsqrt(jnp.maximum(var, 0.0) + 1e-05) * gain_col
        mean = stat[p, 0][:, 0:1] + d_mean
        return scale, bias_col - mean * scale

    row_f = iota((prow, cols), 0).astype(F32)
    col_f = iota((prow, cols), 1).astype(F32)
    flat = gauss(row_f, prow) * gauss(col_f, cols)

    def score_plane(p, i, index, scale, offset, code=None):
        blocks = []
        for pair in range(prow // 2):
            y = conv[p, i, :, 2 * pair * cols : (2 * pair + 2) * cols] * scale + offset
            y = jnp.maximum(y, 0.01 * y)
            big = y.astype(BF)
            small = (y - big.astype(F32)).astype(BF)
            logits = jnp.dot(
                head2, jnp.concatenate([big, small], axis=0), preferred_element_type=F32
            ) + head_bias
            groups = [logits[j : j + 8] for j in range(0, heads, 8)]
            top = functools.reduce(jnp.maximum, groups)
            top = jnp.maximum(top, pltpu.roll(top, 4, 0))
            exps = [jnp.exp(v - top) for v in groups]
            total = functools.reduce(jnp.add, exps)
            total = total + pltpu.roll(total, 4, 0)
            inverse = 1.0 / total
            probs = jnp.concatenate([v * inverse for v in exps], axis=0)
            blocks += [probs[:, :cols], probs[:, cols:]]
        tall = jnp.concatenate(blocks, axis=0)
        big = tall.astype(BF)
        small = (tall - big.astype(F32)).astype(BF)
        summed = jnp.dot(
            gather, jnp.concatenate([big, small], axis=0), preferred_element_type=F32
        )
        index = lax.convert_element_type(index, F32)
        keep = keep_ref[0, p].astype(F32)
        window = gauss(jnp.full((prow, cols), index, F32), PATCH_X) * flat * keep
        share = window * (1.0 / folds)
        for k in range(classes):
            wpad[p, i, k] = summed[k * prow : (k + 1) * prow] * share
        wpad[p, i, classes] = window
        if code is not None:
            coded = (summed * (LEVELS / folds) + 0.5).astype(jnp.int32) - LEVELS // 2
            for k in range(classes // 2):
                codes[p, code, k] = coded[2 * k * prow : 2 * (k + 1) * prow].astype(jnp.int16)

    def slot_of(p, j):
        if RIM < j < RIM + planes - 1:
            return j - RIM - 1
        i = j - starts[p]
        if j <= RIM:
            return jnp.where(i >= 0, inner + i, PATCH_X)
        return jnp.where(i < PATCH_X, i, PATCH_X)

    def send_edges(p):
        for j in range(EDGE):
            snd_lo[p, j] = codes[p, slot_of(p, j) - inner]
            snd_hi[p, j] = codes[p, slot_of(p, RIM + planes - 1 + j) - inner]

        @pl.when(has_right)
        def _():
            remote(snd_hi.at[p], rcv_below.at[p], edge, 2 * p, right).start()

        @pl.when(has_left)
        def _():
            remote(snd_lo.at[p], rcv_above.at[p], edge, 2 * p + 1, left).start()

    shape = (prow, cols)
    count = jnp.full(shape, acq[0].astype(F32), F32)
    step = planes / jnp.maximum(count - 1.0, 1.0)
    anchor = jnp.full(shape, (me * planes).astype(F32), F32)
    last = (slabs * planes - 1) * 1.0
    for slot in range(MOST_ACQ):
        position = jnp.clip(anchor + (slot * step - 0.5), 0.0, last) - anchor
        for e in range(planes + 2):
            value = jnp.maximum(0.0, 1.0 - jnp.abs(position - (e - 1.0)))
            coef[slot, e] = jnp.where(count > slot, value, 0.0)

    for p in range(patches):
        conv_plane(p, 0, RIM + 1)
        shift_of(p)
        add_stats(p, 0)

    @pl.loop(1, inner)
    def _(i):
        for p in range(patches):
            conv_plane(p, i, RIM + 1 + i)
            add_stats(p, i)

    def take_before():
        @pl.when(has_left)
        def _():
            remote(feat_in.at[:, planes - RIM :], before, halo, 0, left).wait_recv()
            remote(meta_hi, meta_below, halo, 2, left).wait_recv()

        lay_planes(before, 0, 0, RIM, True)

    def take_after():
        @pl.when(has_right)
        def _():
            remote(feat_in.at[:, :RIM], after, halo, 1, right).wait_recv()
            remote(meta_lo, meta_above, halo, 3, right).wait_recv()

        lay_planes(after, 0, RIM + planes, RIM, True)

    @pl.when(me % 2 == 0)
    def _():
        take_after()
        take_before()

    @pl.when(me % 2 == 1)
    def _():
        take_before()
        take_after()


    def conv_rest(p, t):
        conv_plane(p, inner + t, starts[p] + rest_index(p, t))
        add_stats(p, inner + t)

    def score_rest(p, t, norms):
        score_plane(p, inner + t, rest_index(p, t), *norms, code=t)

    @pl.loop(0, rest)
    def _(t):
        conv_rest(0, t)

    norms = []
    for p in range(patches):
        norms.append(affine(p))

        if p + 1 < patches:

            @pl.loop(0, rest)
            def _(t, p=p):
                conv_rest(p + 1, t)
                score_rest(p, t, norms[p])
        else:

            @pl.loop(0, rest // 2)
            def _(t, p=p):
                score_rest(p, 2 * t, norms[p])
                score_rest(p, 2 * t + 1, norms[p])
            if rest % 2:
                score_rest(p, rest - 1, norms[p])

        send_edges(p)

    @pl.loop(0, inner)
    def _(i):
        for p in range(patches):
            score_plane(p, i, RIM + 1 + i - starts[p], *norms[p])

    for p in range(patches):

        @pl.when(has_right)
        def _():
            remote(snd_hi.at[p], rcv_below.at[p], edge, 2 * p, right).wait_send()
            remote(snd_lo.at[p], rcv_above.at[p], edge, 2 * p + 1, right).wait_recv()

        @pl.when(has_left)
        def _():
            remote(snd_lo.at[p], rcv_above.at[p], edge, 2 * p + 1, left).wait_send()
            remote(snd_hi.at[p], rcv_below.at[p], edge, 2 * p, left).wait_recv()

        ends = [(e, rcv_below, meta_below, e) for e in range(EDGE)]
        ends += [(planes + 2 - EDGE + j, rcv_above, meta_above, j) for j in range(EDGE)]

        def total(e, k):
            value = wpad[p, slot_of(p, e + RIM - 1), k]
            for plane, codes_in, meta, j in ends:
                if plane == e:
                    window = meta[p, j : j + 1, :] * flat
                    if k < classes:
                        half_at = (k % 2) * prow
                        got = codes_in[p, j, k // 2].astype(F32)[half_at : half_at + prow]
                        window = window * (got * (1.0 / LEVELS) + (LEVELS // 2) / LEVELS)
                    value = value + window
            return value

        inverses = [1.0 / (total(e, classes) + PRIOR) for e in range(planes + 2)]
        for k in range(classes):
            merged = []
            for e in range(planes + 2):
                value = total(e, k)
                if k == 0:
                    value = value + PRIOR
                merged.append(value * inverses[e])
            for slot in range(MOST_ACQ):
                value = coef[slot, 0] * merged[0]
                for e in range(1, planes + 2):
                    value = value + coef[slot, e] * merged[e]
                out[k, slot, p * prow : (p + 1) * prow, :] = value

    @pl.when(has_right)
    def _():
        halo_right.wait_send()
        meta_right.wait_send()

    @pl.when(has_left)
    def _():
        halo_left.wait_send()
        meta_left.wait_send()


def local(features, conv_weight, norm_gain, norm_bias, head_weight, head_bias, patch_offsets, fg_mask, acq_counts):
    channels, planes, rows, cols = features.shape
    folds, classes, _ = head_weight.shape
    patches = patch_offsets.shape[1]
    prow = rows // patches
    wide = folds * channels
    span = planes + 2 * RIM
    vmem = pl.BlockSpec(memory_space=pltpu.VMEM)
    smem = pl.BlockSpec(memory_space=pltpu.SMEM)
    hbm = pl.BlockSpec(memory_space=pltpu.MemorySpace.HBM)
    edges = pltpu.VMEM((patches, EDGE, classes // 2, 2 * prow, cols), jnp.int16)
    meta = pltpu.VMEM((patches, 8, cols), F32)
    rest = PATCH_X - (planes - 2)
    operands = (
        features, jnp.swapaxes(conv_weight, 1, 2), norm_gain, norm_bias,
        jnp.swapaxes(head_weight, 0, 1), head_bias,
    )
    cells = PATCH_X * prow * cols * patches
    return pl.pallas_call(
        kernel,
        out_shape=jax.ShapeDtypeStruct((classes, MOST_ACQ, rows, cols), F32),
        in_specs=[hbm] * 6 + [smem] * 3,
        out_specs=vmem,
        scratch_shapes=[
            *[pltpu.VMEM(value.shape, value.dtype) for value in operands],
            pltpu.VMEM((channels, RIM, rows, cols), BF),
            pltpu.VMEM((channels, RIM, rows, cols), BF),
            pltpu.VMEM((patches, span + 2, (prow + 2) * 3 * channels, cols), BF),
            pltpu.VMEM((wide, 27 * channels), BF),
            pltpu.VMEM((patches, PATCH_X, wide, prow * cols), F32),
            pltpu.VMEM((patches, PATCH_X + 1, classes + 1, prow, cols), F32),
            pltpu.VMEM((patches, rest + 1, classes // 2, 2 * prow, cols), jnp.int16),
            edges, edges, edges, edges,
            meta, meta, meta, meta,
            pltpu.VMEM((patches, 3, wide, cols), F32),
            pltpu.VMEM((MOST_ACQ, planes + 2, prow, cols), F32),
            pltpu.SemaphoreType.DMA((6,)),
            pltpu.SemaphoreType.DMA((4,)),
            pltpu.SemaphoreType.DMA((4,)),
            pltpu.SemaphoreType.DMA((2 * patches,)),
            pltpu.SemaphoreType.DMA((2 * patches,)),
        ],
        compiler_params=pltpu.CompilerParams(
            collective_id=0, has_side_effects=True, vmem_limit_bytes=56 * 1024 * 1024
        ),
        cost_estimate=pl.CostEstimate(
            flops=2 * cells * wide * 27 * channels,
            bytes_accessed=2 * features.size + 4 * classes * MOST_ACQ * rows * cols,
            transcendentals=cells * folds * classes,
        ),
    )(*operands, patch_offsets, fg_mask, acq_counts)


def solution(mesh):
    whole = P(None, ("brain", "slab"), None, None)
    by_slab = P(("brain", "slab"), None)
    in_specs = (whole, P(), P(), P(), P(), P(), by_slab, by_slab, P(("brain", "slab")))
    return jax.shard_map(local, mesh=mesh, in_specs=in_specs, out_specs=whole, check_vma=False)
```
